32 devices in a mesh: head: 4 (over y, x), tok: 8 (over z, core).
Axes of the slice: x: 2, y: 2, z: 4, core: 2. Of those that a mesh axis runs over, the one named last changes fastest.
Arguments:
- stream_one: bfloat16 [16384, 1024], P('tok', 'head'), may hold values from -6 to 6
- stream_two: bfloat16 [16384, 1024], P('tok', 'head'), may hold values from -6 to 6
- buckets: int32 [16384, 4], P('tok'), may hold values from 0 to 703, all different within a row; in each aligned block of 2048 rows (0 to 2047, 2048 to 4095, ...) at most 16 rows name the same one
- lengths: int32 [2], replicated, may hold values from 1024 to 15360, as said below
- gain_attn: bfloat16 [1024], P('head'), may hold values from 0.25 to 1.75
- bias_attn: bfloat16 [1024], P('head'), may hold values from -1.75 to 1.75
- qk_weight: bfloat16 [1024, 1024], P('tok', 'head'), may hold values from -0.25 to 0.25
- value_weight: bfloat16 [1024, 1024], P('tok', 'head'), may hold values from -0.1875 to 0.1875
- out_weight: bfloat16 [1024, 1024], P('head', 'tok'), may hold values from -1.5 to 1.5
- gain_ffn: bfloat16 [1024], P('head'), may hold values from 0.25 to 1.75
- bias_ffn: bfloat16 [1024], P('head'), may hold values from -1.75 to 1.75
- in_weight: bfloat16 [1024, 4096], P('tok', 'head'), may hold values from -0.1875 to 0.1875
- in_bias: bfloat16 [4096], P('head'), may hold values from -3 to 3
- down_weight: bfloat16 [4096, 1024], P('head', 'tok'), may hold values from -0.125 to 0.125
- down_bias: bfloat16 [1024], P('head'), may hold values from -1.75 to 1.75
- cotangent_one: bfloat16 [16384, 1024], P('tok', 'head'), may hold values from -6 to 6
- cotangent_two: bfloat16 [16384, 1024], P('tok', 'head'), may hold values from -6 to 6
Outputs:
- result_one: bfloat16 [16384, 1024], P('tok', 'head')
- result_two: bfloat16 [16384, 1024], P('tok', 'head')
- grad_one: bfloat16 [16384, 1024], P('tok', 'head')
- grad_two: bfloat16 [16384, 1024], P('tok', 'head')
- grad_gain_attn: float32 [1024], P(('head', 'tok'))
- grad_bias_attn: float32 [1024], P(('head', 'tok'))
- grad_qk: float32 [1024, 1024], P('tok', 'head')
- grad_value: float32 [1024, 1024], P('tok', 'head')
- grad_out: float32 [1024, 1024], P('head', 'tok')
- grad_gain_ffn: float32 [1024], P(('head', 'tok'))
- grad_bias_ffn: float32 [1024], P(('head', 'tok'))
- grad_in_weight: float32 [1024, 4096], P('tok', 'head')
- grad_in_bias: float32 [4096], P(('head', 'tok'))
- grad_down_weight: float32 [4096, 1024], P('head', 'tok')
- grad_down_bias: float32 [1024], P(('head', 'tok'))
- bucket_counts: int32 [704], P('tok')
The draws below stay inside these ranges and needn't reach their ends.
Inputs may be any that keep to these rules, and one draw needn't show every extreme that they name: Each token names 4 different buckets; in each aligned block of 2048 tokens no bucket is named by more than 16 tokens. Two sequences packed in order, lengths summing to 16384; the shorter has fewer than 2048 tokens.
All inputs are finite; a program needn't handle non-finite values.
Results may differ from the reference program's by a relative error of at most 0.012.
The reference program's roundings to bfloat16 on the way count: a program that leaves them out, or rounds other values in their place, can miss the bound.
Values may be sent and summed in bfloat16 or wider, within the bound.
No kernel may reach another device: no remote copies, remote signals or barrier semaphores. Data moves between devices by JAX's collectives and lax.ppermute only.
A program may use at most 256 MiB of HBM per device.

```python
import math
import jax
import jax.numpy as jnp
import numpy as np
from jax import lax

D = 1024
H = 8
DH = 128
FF = 4096
ROUNDS = 4
CAP = 128
MIN_LEN = 1024
TOK_DEV = 2048
MOST = 16
NB = 704
TOKENS = 16384
N_TOK = 8


def draw_lengths(key, part):
    key = jax.random.fold_in(key, 17)
    short_key, order_key = jax.random.split(key)
    shorter = jax.random.randint(short_key, (), MIN_LEN, TOK_DEV)
    longer = TOKENS - shorter
    swapped = jax.random.randint(order_key, (), 0, 2)
    return jnp.where(swapped == 0, jnp.stack([longer, shorter]), jnp.stack([shorter, longer])).astype(jnp.int32)


def steps_of(key, extent, cuts, least, top_value):
    gain, own = 1.0, jax.random.fold_in(key, 6)
    for position, parts in cuts:
        draws = jnp.exp(jax.random.uniform(jax.random.fold_in(own, position), (parts,), jnp.float32, least / len(cuts), top_value / len(cuts)))
        gain = gain * jnp.repeat(draws, extent[position] // parts).reshape([-1 if axis == position else 1 for axis in range(len(extent))])
    return gain


def deal_out(key, own, number, rows, number_of, top, most, slope):
    ranking = jax.random.permutation(key, number_of)
    packed, usual = load_shares(number_of, rows * top, most, slope, True), load_shares(number_of, rows * top, most, slope, False)
    places = jnp.arange(number_of)

    def named(tallies, offset_by):
        used = int((tallies > 0).sum())
        fixed = max(1, used // 4)
        shifted = fixed + (places - fixed + offset_by * (used - fixed)) % max(1, number_of - fixed)
        return jnp.zeros((number_of,), jnp.int32).at[ranking[jnp.where(places < fixed, places, shifted)]].set(jnp.asarray(tallies, jnp.int32))

    tallies = jnp.where(number % 4 == 0, named(packed, number // 4), named(usual, number - number // 4 - 1))
    mixed = jax.random.permutation(jax.random.fold_in(own, 3), number_of)
    giver, taker = mixed[0:number_of // 2 * 2:2], mixed[1:number_of // 2 * 2:2]
    slack = jnp.minimum(tallies[giver] - 1, most - tallies[taker]) // 2
    slack = jnp.where((giver == ranking[0]) | (taker == ranking[0]) | (tallies[taker] == 0), 0, jnp.maximum(slack, 0))
    shifted = jax.random.randint(jax.random.fold_in(own, 4), (number_of // 2,), 0, 1 << 20) % (slack + 1)
    tallies = tallies.at[giver].add(-shifted).at[taker].add(shifted)
    labels = jnp.searchsorted(jnp.cumsum(tallies), jnp.arange(rows * top), side="right").astype(jnp.int32)
    table = labels.reshape(top, rows).T
    table = table[jax.random.permutation(jax.random.fold_in(own, 1), rows)]
    offset_by = jax.random.randint(jax.random.fold_in(own, 2), (rows, 1), 0, top)
    return jnp.take_along_axis(table, (jnp.arange(top)[None, :] + offset_by) % top, axis=1)


def load_shares(number_of, total, most, skew, full):
    loads = [(1 << 20) // math.isqrt(rank ** skew) + 1 for rank in range(1, number_of + 1)]
    largest = most if full else min(most, max(-(-total // number_of), total * loads[0] // sum(loads)))
    least = 1 if total - largest >= number_of - 1 else 0
    holding, spare = [largest] + [least] * (number_of - 1), total - largest - least * (number_of - 1)
    while spare > 0:
        movable = [i for i in range(1, number_of) if holding[i] < largest] or [i for i in range(1, number_of) if holding[i] < most]
        mass, budget = sum([loads[i] for i in movable]), spare
        for i in movable:
            extra = min(most - holding[i], max(1, budget * loads[i] // mass), spare)
            holding[i] = holding[i] + extra
            spare = spare - extra
    return np.array(holding)


def scatter_about(rng, shape, scale, bound, shards=(), kind=jnp.bfloat16):
    drawn = jax.random.normal(rng, shape, jnp.float32) * scale
    if len(shards) > 0:
        drawn = steps_of(rng, shape, shards, -0.22, 0.18) * drawn
    return jnp.clip(drawn, min=-bound, max=bound).astype(kind)


def setup_inputs(seed: int = 0) -> dict:
    key_of = jax.random.split(jax.random.key(seed), 18)
    stream_one = scatter_about(key_of[0], (TOKENS, D), 1.0, 6.0, ((0, 8), (1, 4)))
    stream_two = scatter_about(key_of[1], (TOKENS, D), 1.0, 6.0, ((0, 8), (1, 4)))
    buckets_keys = jax.random.split(jax.random.fold_in(key_of[2], 1), TOKENS // TOK_DEV)
    buckets_turns = jax.random.permutation(jax.random.fold_in(key_of[2], 3), TOKENS // TOK_DEV)
    buckets = jax.vmap(lambda own, number: deal_out(jax.random.fold_in(key_of[2], 2), own, number, TOK_DEV, NB, ROUNDS, MOST, 2))(buckets_keys, buckets_turns).reshape((TOKENS, ROUNDS))
    lengths = draw_lengths(jax.random.fold_in(key_of[17], 71), 0)
    gain_attn = jnp.clip(1.0 + 0.15 * jax.random.normal(key_of[4], (D,), jnp.float32), 0.25, 1.75).astype(jnp.bfloat16)
    bias_attn = scatter_about(key_of[5], (D,), 0.3, 1.75, ((0, 4),))
    qk_weight = scatter_about(key_of[6], (D, D), (D // 2) ** -0.5, 0.25, ((0, 8), (1, 4)))
    value_weight = scatter_about(key_of[7], (D, D), D ** -0.5, 0.1875, ((0, 8), (1, 4)))
    out_weight = scatter_about(key_of[8], (D, D), (D // 64) ** -0.5, 1.5, ((0, 4), (1, 8)))
    gain_ffn = jnp.clip(1.0 + 0.15 * jax.random.normal(key_of[9], (D,), jnp.float32), 0.25, 1.75).astype(jnp.bfloat16)
    bias_ffn = scatter_about(key_of[10], (D,), 0.3, 1.75, ((0, 4),))
    in_weight = scatter_about(key_of[11], (D, FF), D ** -0.5, 0.1875, ((0, 8), (1, 4)))
    in_bias = scatter_about(key_of[12], (FF,), 0.5, 3.0, ((0, 4),))
    down_weight = scatter_about(key_of[13], (FF, D), (FF // 2) ** -0.5, 0.125, ((0, 4), (1, 8)))
    down_bias = scatter_about(key_of[14], (D,), 0.3, 1.75, ((0, 4),))
    cotangent_one = scatter_about(key_of[15], (TOKENS, D), 1.0, 6.0, ((0, 8), (1, 4)))
    cotangent_two = scatter_about(key_of[16], (TOKENS, D), 1.0, 6.0, ((0, 8), (1, 4)))
    return {"stream_one": stream_one, "stream_two": stream_two, "buckets": buckets, "lengths": lengths, "gain_attn": gain_attn, "bias_attn": bias_attn, "qk_weight": qk_weight, "value_weight": value_weight, "out_weight": out_weight, "gain_ffn": gain_ffn, "bias_ffn": bias_ffn, "in_weight": in_weight, "in_bias": in_bias, "down_weight": down_weight, "down_bias": down_bias, "cotangent_one": cotangent_one, "cotangent_two": cotangent_two}


@jax.custom_vjp
def low(v):
    return lax.optimization_barrier(v.astype(jnp.bfloat16)).astype(jnp.float32)

@jax.custom_vjp
def low_back(v):
    return v

def low_keep(v):
    return (low(v), None)

def low_pass(kept, grad):
    return (grad,)

def back_keep(v):
    return (v, None)

def back_low(kept, grad):
    return (low(grad),)
low.defvjp(low_keep, low_pass)
low_back.defvjp(back_keep, back_low)
HIGHEST = lax.Precision.HIGHEST
SELF_SCORE = -10000.0
MASKED = -1000000000.0

def product(left_side, right_side):
    return jnp.dot(left_side, right_side, precision=HIGHEST)

def layer_norm(row_block, gain_vec, bias_vec):
    row_mean = lax.optimization_barrier(jnp.mean(row_block, axis=1, keepdims=True))
    centred = row_block - row_mean
    row_scale = lax.rsqrt(lax.optimization_barrier(jnp.mean(centred * centred, axis=1, keepdims=True)) + 1e-05)
    return centred * row_scale * gain_vec + bias_vec

def block_ranks(chosen):
    flat_ids = chosen.reshape(-1)
    length_all = flat_ids.shape[0]
    positions = jnp.arange(length_all, dtype=jnp.int32)
    sorted_at = jnp.argsort(flat_ids * length_all + positions)
    ordered = flat_ids[sorted_at]
    starts = jnp.concatenate([jnp.ones((1,), dtype=bool), ordered[1:] != ordered[:-1]])
    run_start = lax.cummax(jnp.where(starts, positions, 0), axis=0)
    rank_of = jnp.zeros((length_all,), jnp.int32).at[sorted_at].set(positions - run_start)
    return rank_of.reshape(chosen.shape)

def score_mask(places, boundary):
    query_place = places[:, :, None]
    key_place = places[:, None, :]
    same_seq = (query_place >= boundary) == (key_place >= boundary)
    allowed = (key_place >= 0) & same_seq & (key_place < query_place)
    itself = key_place == query_place
    return (allowed, itself)

def bucket_group(queries, values, places, boundary):
    inverse = lax.rsqrt(lax.optimization_barrier(jnp.sum(queries * queries, axis=2, keepdims=True)) + 1e-06)
    unit_keys = low(queries * inverse)
    scores = low_back(jnp.einsum('gqd,gkd->gqk', queries, unit_keys, precision=HIGHEST))
    allowed, itself = score_mask(places, boundary)
    scores = jnp.where(allowed, scores, jnp.where(itself, SELF_SCORE, MASKED))
    highest = lax.optimization_barrier(jnp.max(scores, axis=2, keepdims=True))
    totals = highest + jnp.log(lax.optimization_barrier(jnp.sum(jnp.exp(scores - highest), axis=2, keepdims=True)))
    probability = low(jnp.exp(scores - totals))
    mixture = low_back(jnp.einsum('gqk,gkd->gqd', probability, values, precision=HIGHEST))
    return (mixture, totals[:, :, 0])

def lsh_attention(shared, values, slot_token, places, slot_of, boundary):
    group_size = max(1, 512 // CAP)
    head_shared = shared.reshape(TOKENS, H, DH).transpose(1, 0, 2)
    head_values = values.reshape(TOKENS, H, DH).transpose(1, 0, 2)
    token_groups = slot_token.reshape(-1, group_size, CAP)
    place_groups = places.reshape(-1, group_size, CAP)

    def one_head(couple):
        queries_all, values_all = couple
        padded_q = jnp.concatenate([queries_all, jnp.zeros((1, DH), queries_all.dtype)], axis=0)
        padded_v = jnp.concatenate([values_all, jnp.zeros((1, DH), values_all.dtype)], axis=0)

        def one_group(pieces):
            chosen, where_from = pieces
            return bucket_group(padded_q[chosen], padded_v[chosen], where_from, boundary)
        mixture, totals = lax.map(jax.checkpoint(one_group), (token_groups, place_groups))
        mixture = mixture.reshape(NB * CAP, DH)
        totals = totals.reshape(NB * CAP)
        per_round = mixture[slot_of]
        weights = jax.nn.softmax(totals[slot_of], axis=1)
        return lax.optimization_barrier(jnp.sum(weights[:, :, None] * per_round, axis=1))
    head_out = lax.map(jax.checkpoint(one_head), (head_shared, head_values))
    return head_out.transpose(1, 0, 2).reshape(TOKENS, D)

def reference(stream_one, stream_two, buckets, lengths, gain_attn, bias_attn, qk_weight, value_weight, out_weight, gain_ffn, bias_ffn, in_weight, in_bias, down_weight, down_bias, cotangent_one, cotangent_two):
    blocks = buckets.reshape(N_TOK, TOK_DEV, ROUNDS)
    rank_of = jax.vmap(block_ranks)(blocks).reshape(TOKENS, ROUNDS)
    block_index = (jnp.arange(TOKENS, dtype=jnp.int32) // TOK_DEV)[:, None]
    slot_of = (buckets * CAP + block_index * MOST + rank_of).astype(jnp.int32)
    owners = jnp.repeat(jnp.arange(TOKENS, dtype=jnp.int32), ROUNDS)
    slot_token = jnp.full((NB * CAP,), TOKENS, jnp.int32).at[slot_of.reshape(-1)].set(owners)
    places = jnp.where(slot_token < TOKENS, slot_token, -1).astype(jnp.int32)
    boundary = lengths[0]
    bucket_counts = jnp.zeros((NB,), jnp.int32).at[buckets.reshape(-1)].add(1)

    def whole_layer(left_stream, right_stream, gain_a, bias_a, weight_qk, weight_v, weight_o, gain_f, bias_f, weight_in, bias_up, weight_down, bias_down):
        normed = low(layer_norm(right_stream, gain_a, bias_a))
        shared = low(low_back(product(normed, weight_qk)))
        values = low(low_back(product(normed, weight_v)))
        attended = low(lsh_attention(shared, values, slot_token, places, slot_of, boundary))
        first_out = left_stream + low_back(product(attended, weight_o))
        normed_two = low(layer_norm(low(first_out), gain_f, bias_f))
        hidden = low(jax.nn.gelu(low_back(product(normed_two, weight_in) + bias_up), approximate=True))
        second_out = right_stream + low_back(product(hidden, weight_down) + bias_down)
        return (first_out, second_out)
    floats = jax.tree.map(lambda tensor: tensor.astype(jnp.float32), (stream_one, stream_two, gain_attn, bias_attn, qk_weight, value_weight, out_weight, gain_ffn, bias_ffn, in_weight, in_bias, down_weight, down_bias))
    outputs, pullback = jax.vjp(whole_layer, *floats)
    gradients = pullback((cotangent_one.astype(jnp.float32), cotangent_two.astype(jnp.float32)))
    return (outputs[0].astype(jnp.bfloat16), outputs[1].astype(jnp.bfloat16), gradients[0].astype(jnp.bfloat16), gradients[1].astype(jnp.bfloat16), gradients[2], gradients[3], gradients[4], gradients[5], gradients[6], gradients[7], gradients[8], gradients[9], gradients[10], gradients[11], gradients[12], bucket_counts)
```

```python
import jax
import jax.numpy as jnp
from jax import lax
from jax.experimental import pallas as pl
from jax.experimental.pallas import tpu as pltpu
from jax.sharding import PartitionSpec as P

DH = 128
CAP = 128
HALF = 64
GROUP = 128
ROWS = 256

SELF_SCORE = -10000.0
MASKED = -1000000000.0
NOTHING = -1e30
LOWEST = -3e38
PENALTY = 1048576.0
F32 = jnp.float32
BF16 = jnp.bfloat16
VMEM_BYTES = 60 * 1024 * 1024


def round_up(value, multiple):
    return -(-value // multiple) * multiple


def iota(shape, axis):
    return lax.broadcasted_iota(jnp.int32, shape, axis)


def dot_nt(left, right):
    return lax.dot_general(left, right, (((1,), (1,)), ((), ())), preferred_element_type=F32)


def dot_tn(left, right):
    return lax.dot_general(left, right, (((0,), (0,)), ((), ())), preferred_element_type=F32)


def dot_nn(left, right):
    return jnp.dot(left, right, preferred_element_type=F32)


def split_three(value):
    high = value.astype(BF16)
    rest = value - high.astype(F32)
    middle = rest.astype(BF16)
    return high, middle, (rest - middle.astype(F32)).astype(BF16)


def column_to_row(column):
    spread = jnp.broadcast_to(column, (GROUP, GROUP))
    same = iota((GROUP, GROUP), 0) == iota((GROUP, GROUP), 1)
    return jnp.sum(jnp.where(same, spread, 0.0), axis=0, keepdims=True)


def row_to_column(row):
    spread = jnp.broadcast_to(row, (GROUP, GROUP))
    same = iota((GROUP, GROUP), 0) == iota((GROUP, GROUP), 1)
    return jnp.sum(jnp.where(same, spread, 0.0), axis=1, keepdims=True)


class Plan:
    def __init__(self, blocks, tokens, most, buckets):
        self.blocks, self.tokens, self.most, self.buckets = blocks, tokens, most, buckets
        self.rows = round_up(buckets, 16)
        self.tiles = -(-buckets // HALF)
        self.pitch = self.tiles * HALF
        self.per_step = next(n for n in (16, 8, 4, 2, 1) if buckets % n == 0)
        self.steps = buckets // self.per_step
        self.deep = self.tiles * most * HALF
        self.together = next(n for n in (4, 2, 1) if most % n == 0)
        self.chunk = min(tokens, 512)


def ranks_by_bucket(plan, named_ref, base, block, boundary, rank_ref):
    wide = ROWS
    row = iota((plan.rows, 1), 0)
    ids = jnp.where(row < plan.buckets, (row + base).astype(F32), -100.0)
    earlier = jnp.where(iota((wide, wide), 0) < iota((wide, wide), 1), 1.0, 0.0).astype(BF16)
    count = jnp.zeros((plan.rows, 1), F32)
    below = jnp.zeros((plan.rows, 1), F32)
    for part in range(plan.tokens // wide):
        cols = slice(part * wide, (part + 1) * wide)
        member = ids == named_ref[0, 0:1, cols]
        for r in range(1, 4):
            member = member | (ids == named_ref[0, r : r + 1, cols])
        ones = jnp.where(member, 1.0, 0.0)
        before = dot_nn(ones.astype(BF16), earlier)
        rank_ref[:, cols] = jnp.where(member, before + count, -1.0)
        place = block * plan.tokens + part * wide + iota((1, wide), 1)
        below = below + jnp.sum(jnp.where(place < boundary, ones, 0.0), axis=1, keepdims=True)
        count = count + jnp.sum(ones, axis=1, keepdims=True)
    return count, below


def ranks_by_token(plan, named_ref, base, rank_ref):
    wide = ROWS
    lane = iota((1, GROUP), 1) % HALF
    later = jnp.where(iota((wide, wide), 1) < iota((wide, wide), 0), 1.0, 0.0).astype(BF16)
    names = jnp.transpose(named_ref[0])
    count = [jnp.zeros((1, GROUP), F32) for _ in range(plan.tiles)]
    for part in range(plan.tokens // wide):
        rows = slice(part * wide, (part + 1) * wide)
        named = [jnp.broadcast_to(names[rows, r : r + 1], (wide, GROUP)) for r in range(4)]
        for tile in range(plan.tiles):
            bucket = lane + tile * HALF
            ids = jnp.where(bucket < plan.buckets, (bucket + base).astype(F32), -100.0)
            member = ids == named[0]
            for r in range(1, 4):
                member = member | (ids == named[r])
            ones = jnp.where(member, 1.0, 0.0)
            before = dot_nn(later, ones.astype(BF16))
            rank_ref[rows, tile * GROUP : (tile + 1) * GROUP] = jnp.where(
                member, before + count[tile], -1.0
            )
            count[tile] = count[tile] + jnp.sum(ones, axis=0, keepdims=True)


def gather_rows(plan, rank_ref, table, block, left_ref, right_ref):
    def some(turn, _):
        ranks = rank_ref[...]
        picks = [
            jnp.where(ranks == (turn * plan.together + n).astype(F32), 1.0, 0.0).astype(BF16)
            for n in range(plan.together)
        ]
        found = dot_nn(jnp.concatenate(picks, axis=0), table)
        for n in range(plan.together):
            start = pl.multiple_of((block * plan.most + turn * plan.together + n) * plan.pitch, 8)
            part = found[n * plan.rows : (n + 1) * plan.rows]
            left_ref[pl.ds(start, plan.rows), :] = part[:, :DH]
            right_ref[pl.ds(start, plan.rows), :] = part[:, DH:]
        return 0

    lax.fori_loop(0, plan.most // plan.together, some, 0)


def clear_padding(plan, refs):
    extra = plan.pitch - plan.rows
    if extra == 0:
        return

    def one(slot, _):
        start = pl.multiple_of(slot * plan.pitch + plan.rows, 8)
        for ref in refs:
            ref[pl.ds(start, extra), :] = jnp.zeros((extra, DH), F32)
        return 0

    lax.fori_loop(0, CAP, one, 0)


def block_rows(plan, slot_ref, block, out_ref, cols):
    for tile in range(plan.tiles):
        for k in range(plan.most):
            start = pl.multiple_of((block * plan.most + k) * plan.pitch + tile * HALF, 8)
            to = (tile * plan.most + k) * HALF
            out_ref[to : to + HALF, cols] = slot_ref[pl.ds(start, HALF), :].astype(BF16)


def pair_values(j):
    return jnp.where(iota((1, GROUP), 1) < HALF, 2.0 * j, 2.0 * j + 1.0)


def forward_body(
    plan, scal, named_ref, shared_ref, value_ref, slot_shared, slot_value, out_ref,
    left_ref, right_ref, rank_ref, token_rank, code_ref, total_ref, lhs_ref, rhs_ref, lse_ref,
):
    step = pl.program_id(0)
    boundary, base = scal[0], scal[1]
    first_scatter = plan.blocks + plan.steps

    @pl.when(step == 0)
    def _():
        code_ref[...] = jnp.zeros_like(code_ref)
        clear_padding(plan, (left_ref, right_ref))

    @pl.when(step < plan.blocks)
    def _():
        block = scal[2 + jnp.minimum(step, plan.blocks - 1)]
        count, below = ranks_by_bucket(plan, named_ref, base, block, boundary, rank_ref)
        nth = iota((plan.rows, CAP), 1) - block * plan.most
        valid = (nth >= 0) & (nth < plan.most) & (nth.astype(F32) < count)
        code_ref[...] = jnp.where(
            valid, jnp.where(nth.astype(F32) < below, 1.0, 2.0), code_ref[...]
        )
        table = jnp.concatenate([shared_ref[0], value_ref[0]], axis=1)
        gather_rows(plan, rank_ref, table, block, left_ref, right_ref)

    @pl.when(step == plan.blocks)
    def _():
        code = code_ref[...]
        slot = iota((plan.rows, CAP), 1).astype(F32)
        change = jnp.min(jnp.where(code == 2.0, slot, 1.0 * CAP), axis=1, keepdims=True)
        code_ref[...] = jnp.where(
            code == 0.0, 0.0, jnp.where(code == 1.0, change, 1.0 * CAP)
        )

    @pl.when((step >= plan.blocks) & (step < first_scatter))
    def _():
        first = (step - plan.blocks) * plan.per_step
        row = iota((CAP, CAP), 0)
        col = iota((CAP, CAP), 1)
        batch = 2 if plan.per_step % 2 == 0 else 1

        def some(turn, _):
            at = [first + turn * batch + n for n in range(batch)]
            queries = [left_ref[pl.ds(b, CAP, stride=plan.pitch), :] for b in at]
            values = [right_ref[pl.ds(b, CAP, stride=plan.pitch), :] for b in at]
            limits = [code_ref[pl.ds(b, 1), :] for b in at]
            results = []
            for n in range(batch):
                query = queries[n]
                inverse = lax.rsqrt(jnp.sum(query * query, axis=1, keepdims=True) + 1e-06)
                query_low = query.astype(BF16)
                value_low = values[n].astype(BF16)
                key_low = (query * inverse).astype(BF16)
                scores = dot_nt(query_low, key_low)
                allowed = (row > col) & (row.astype(F32) < limits[n])
                scores = jnp.where(allowed, scores, jnp.where(row == col, SELF_SCORE, MASKED))
                highest = jnp.max(scores, axis=1, keepdims=True)
                raised = jnp.exp(scores - highest)
                summed = jnp.sum(raised, axis=1, keepdims=True)
                weight = (raised * (1.0 / summed)).astype(BF16)
                mixture = dot_nn(weight, value_low)
                results.append((query_low, value_low, mixture, highest + jnp.log(summed)))
            for n in range(batch):
                query_low, value_low, mixture, total = results[n]
                slot_shared[turn * batch + n] = query_low
                slot_value[turn * batch + n] = value_low
                right_ref[pl.ds(at[n], CAP, stride=plan.pitch), :] = mixture
                tile = at[n] // HALF
                mine = (col % HALF) == (at[n] - tile * HALF)
                total_ref[tile] = jnp.where(mine, total, total_ref[tile])
            return 0

        lax.fori_loop(0, plan.per_step // batch, some, 0)

    @pl.when(step >= first_scatter)
    def _():
        block = scal[2 + jnp.maximum(step - first_scatter, 0)]
        ranks_by_token(plan, named_ref, base, token_rank)
        block_rows(plan, right_ref, block, rhs_ref, slice(0, DH))
        pairs = plan.most // 2
        left_half = iota((1, GROUP), 1) < HALF

        def vector(tile, j):
            rows = [
                total_ref[tile, pl.ds(block * plan.most + 2 * j + n, 1), :] for n in range(2)
            ]
            return jnp.where(left_half, rows[0], rows[1])

        def chunk(part, _):
            start = part * plan.chunk
            for sub in range(plan.chunk // GROUP):
                rows = pl.ds(pl.multiple_of(start + sub * GROUP, GROUP), GROUP)
                here = slice(sub * GROUP, (sub + 1) * GROUP)
                totals = []
                for tile in range(plan.tiles):
                    ranks = token_rank[rows, tile * GROUP : (tile + 1) * GROUP]
                    found = jnp.full((GROUP, GROUP), LOWEST, F32)
                    for j in range(pairs):
                        found = jnp.where(ranks == pair_values(j), vector(tile, j), found)
                    totals.append(jnp.maximum(found, pltpu.roll(found, HALF, 1)))
                highest = totals[0]
                for tile in range(1, plan.tiles):
                    highest = jnp.maximum(highest, totals[tile])
                highest = jnp.max(highest, axis=1, keepdims=True)
                weights = [
                    jnp.where(one > 0.1 * LOWEST, jnp.exp(one - highest), 0.0) for one in totals
                ]
                summed = weights[0]
                for tile in range(1, plan.tiles):
                    summed = summed + weights[tile]
                summed = 0.5 * jnp.sum(summed, axis=1, keepdims=True)
                some_here = summed > 0.0
                scale = jnp.where(some_here, 1.0 / jnp.where(some_here, summed, 1.0), 0.0)
                lse = jnp.where(
                    some_here, highest + jnp.log(jnp.where(some_here, summed, 1.0)), NOTHING
                )
                lse_ref[pl.ds(part * (plan.chunk // GROUP) + sub, 1), :] = column_to_row(lse)
                for tile in range(plan.tiles):
                    ranks = token_rank[rows, tile * GROUP : (tile + 1) * GROUP]
                    weight = weights[tile] * scale
                    for j in range(pairs):
                        to = (tile * pairs + j) * GROUP
                        lhs_ref[here, to : to + GROUP] = jnp.where(
                            ranks == pair_values(j), weight, 0.0
                        ).astype(BF16)
            mixed = dot_nn(lhs_ref[...], rhs_ref[...])
            out_ref[0, pl.ds(pl.multiple_of(start, GROUP), plan.chunk), :] = mixed.astype(BF16)
            return 0

        lax.fori_loop(0, plan.tokens // plan.chunk, chunk, 0)
        extra = plan.tokens // GROUP
        for n, piece in enumerate(split_three(lse_ref[...])):
            out_ref[0, plan.tokens + n * extra : plan.tokens + (n + 1) * extra, :] = piece


def forward_call(plan, scal, named, shared, values):
    first_scatter = plan.blocks + plan.steps

    def named_at(i, scal):
        here = jnp.where(i < plan.blocks, i, jnp.maximum(i - first_scatter, 0))
        return (scal[2 + here], 0, 0)

    def table_at(i, scal):
        return (jnp.minimum(i, plan.blocks - 1), 0, 0)

    def slots_at(i, scal):
        return (jnp.clip(i - plan.blocks, 0, plan.steps - 1), 0, 0)

    def out_at(i, scal):
        return (jnp.maximum(i - first_scatter, 0), 0, 0)

    packed = plan.tokens + 3 * (plan.tokens // GROUP)
    slots = jax.ShapeDtypeStruct((plan.buckets, CAP, DH), BF16)
    return pl.pallas_call(
        lambda *refs: forward_body(plan, *refs),
        grid_spec=pltpu.PrefetchScalarGridSpec(
            num_scalar_prefetch=1,
            grid=(plan.blocks + plan.steps + plan.blocks,),
            in_specs=[
                pl.BlockSpec((1, 8, plan.tokens), named_at),
                pl.BlockSpec((1, plan.tokens, DH), table_at),
                pl.BlockSpec((1, plan.tokens, DH), table_at),
            ],
            out_specs=[
                pl.BlockSpec((plan.per_step, CAP, DH), slots_at),
                pl.BlockSpec((plan.per_step, CAP, DH), slots_at),
                pl.BlockSpec((1, packed, DH), out_at),
            ],
            scratch_shapes=[
                pltpu.VMEM((CAP * plan.pitch, DH), F32),
                pltpu.VMEM((CAP * plan.pitch, DH), F32),
                pltpu.VMEM((plan.rows, plan.tokens), F32),
                pltpu.VMEM((plan.tokens, plan.tiles * GROUP), F32),
                pltpu.VMEM((plan.rows, CAP), F32),
                pltpu.VMEM((plan.tiles, CAP, GROUP), F32),
                pltpu.VMEM((plan.chunk, plan.deep), BF16),
                pltpu.VMEM((plan.deep, DH), BF16),
                pltpu.VMEM((plan.tokens // GROUP, GROUP), F32),
            ],
        ),
        out_shape=[slots, slots, jax.ShapeDtypeStruct((plan.blocks, packed, DH), BF16)],
        compiler_params=pltpu.CompilerParams(vmem_limit_bytes=VMEM_BYTES),
        name="bucket_forward",
    )(scal, named, shared, values)


def merge_call(parts):
    count, packed, _ = parts[0].shape
    extra = packed // (GROUP + 3)
    tokens = extra * GROUP

    def body(*refs):
        ins, out_ref = refs[:-1], refs[-1]
        lses = []
        for ref in ins:
            pieces = [
                ref[0, tokens + n * extra : tokens + (n + 1) * extra, :].astype(F32)
                for n in range(3)
            ]
            lses.append(pieces[0] + pieces[1] + pieces[2])
        highest = lses[0]
        for lse in lses[1:]:
            highest = jnp.maximum(highest, lse)
        raised = [jnp.exp(lse - highest) for lse in lses]
        summed = raised[0]
        for one in raised[1:]:
            summed = summed + one
        shares = [one / summed for one in raised]
        for n, piece in enumerate(split_three(highest + jnp.log(summed))):
            out_ref[0, tokens + n * extra : tokens + (n + 1) * extra, :] = piece
        for g in range(extra):
            rows = slice(g * GROUP, (g + 1) * GROUP)
            total = jnp.zeros((GROUP, DH), F32)
            for ref, share in zip(ins, shares):
                total = total + row_to_column(share[g : g + 1, :]) * ref[0, rows, :].astype(F32)
            out_ref[0, rows, :] = total.astype(BF16)

    spec = pl.BlockSpec((1, packed, DH), lambda i: (i, 0, 0))
    return pl.pallas_call(
        body,
        grid=(count,),
        in_specs=[spec] * len(parts),
        out_specs=spec,
        out_shape=jax.ShapeDtypeStruct((count, packed, DH), BF16),
        compiler_params=pltpu.CompilerParams(vmem_limit_bytes=VMEM_BYTES),
        name="merge_rounds",
    )(*parts)


def pack_call(grads, mixed):
    count, tokens, _ = grads.shape
    packed = mixed.shape[1]
    extra = tokens // GROUP

    def body(grad_ref, mixed_ref, out_ref):
        out_ref[0, :tokens, :] = grad_ref[0]
        out_ref[0, tokens:packed, :] = mixed_ref[0, tokens:packed, :]
        rows = []
        for g in range(extra):
            here = slice(g * GROUP, (g + 1) * GROUP)
            product = grad_ref[0, here, :].astype(F32) * mixed_ref[0, here, :].astype(F32)
            rows.append(column_to_row(jnp.sum(product, axis=1, keepdims=True)))
        dots = jnp.concatenate(rows, axis=0)
        high = dots.astype(BF16)
        out_ref[0, packed : packed + extra, :] = high
        out_ref[0, packed + extra : packed + 2 * extra, :] = (dots - high.astype(F32)).astype(BF16)

    full = packed + 2 * extra
    return pl.pallas_call(
        body,
        grid=(count,),
        in_specs=[
            pl.BlockSpec((1, tokens, DH), lambda i: (i, 0, 0)),
            pl.BlockSpec((1, packed, DH), lambda i: (i, 0, 0)),
        ],
        out_specs=pl.BlockSpec((1, full, DH), lambda i: (i, 0, 0)),
        out_shape=jax.ShapeDtypeStruct((count, full, DH), BF16),
        compiler_params=pltpu.CompilerParams(vmem_limit_bytes=VMEM_BYTES),
        name="pack_gradient",
    )(grads, mixed)


def backward_body(
    plan, scal, named_ref, grad_ref, slot_shared, slot_value, shared_out, value_out,
    left_ref, right_ref, rank_ref, token_rank, extra_ref, lhs_ref, rhs_ref,
):
    step = pl.program_id(0)
    boundary, base = scal[0], scal[1]
    first_scatter = plan.blocks + plan.steps
    lane = iota((1, GROUP), 1)

    @pl.when(step == 0)
    def _():
        clear_padding(plan, (left_ref, right_ref))

    @pl.when(step < plan.blocks)
    def _():
        block = scal[2 + jnp.minimum(step, plan.blocks - 1)]
        ranks_by_bucket(plan, named_ref, base, block, boundary, rank_ref)
        groups = plan.tokens // GROUP
        pieces = [
            grad_ref[0, plan.tokens + n * groups : plan.tokens + (n + 1) * groups, :].astype(F32)
            for n in range(5)
        ]
        spread = jnp.where(iota((8, GROUP), 0) == iota((8, GROUP), 1), 1.0, 0.0)
        for g in range(groups):
            place = block * plan.tokens + g * GROUP + lane
            rows = [piece[g : g + 1, :] for piece in pieces]
            rows.append(jnp.where(place < boundary, 1.0, 0.0))
            rows.append(jnp.zeros((2, GROUP), F32))
            columns = jnp.transpose(jnp.concatenate(rows, axis=0))
            extra_ref[g * GROUP : (g + 1) * GROUP, :] = dot_nn(
                columns.astype(BF16), spread.astype(BF16)
            ).astype(BF16)
        table = jnp.concatenate([grad_ref[0, : plan.tokens, :], extra_ref[...]], axis=1)
        gather_rows(plan, rank_ref, table, block, left_ref, right_ref)

    @pl.when((step >= plan.blocks) & (step < first_scatter))
    def _():
        first = (step - plan.blocks) * plan.per_step
        key_slot = iota((CAP, CAP), 0)
        query_slot = iota((CAP, CAP), 1)
        earlier = key_slot < query_slot
        itself = key_slot == query_slot
        query_scale = jnp.where(lane == 5, PENALTY, 1.0)
        query_shift = jnp.where(lane == 5, -PENALTY, 0.0)
        key_scale = jnp.where(lane == 5, 1.0, 0.0)
        key_shift = jnp.where(lane < 3, -1.0, 0.0)
        value_extra = jnp.broadcast_to(
            jnp.where((lane == 3) | (lane == 4), -1.0, 0.0), (CAP, GROUP)
        ).astype(BF16)
        minus_total = jnp.broadcast_to(key_shift, (16, GROUP)).astype(BF16)
        batch = 2 if plan.per_step % 2 == 0 else 1

        def some(turn, _):
            at = [first + turn * batch + n for n in range(batch)]
            grads = [left_ref[pl.ds(b, CAP, stride=plan.pitch), :] for b in at]
            extras = [right_ref[pl.ds(b, CAP, stride=plan.pitch), :] for b in at]
            results = []
            for n in range(batch):
                query = slot_shared[turn * batch + n]
                value = slot_value[turn * batch + n]
                grad, extra = grads[n].astype(BF16), extras[n]
                wide = query.astype(F32)
                inverse = lax.rsqrt(jnp.sum(wide * wide, axis=1, keepdims=True) + 1e-06)
                unit = wide * inverse
                key = unit.astype(BF16)
                extra_low = extra.astype(BF16)
                query_extra = (extra * query_scale + query_shift).astype(BF16)
                key_extra = (extra * key_scale + key_shift).astype(BF16)
                scores = dot_nt(
                    jnp.concatenate([key, key_extra], axis=1),
                    jnp.concatenate([query, query_extra], axis=1),
                )
                slope = dot_nt(
                    jnp.concatenate([value, value_extra], axis=1),
                    jnp.concatenate([grad, extra_low], axis=1),
                )
                own = dot_nt(minus_total, extra_low)[0:1, :] + SELF_SCORE
                scores = jnp.where(earlier, scores, jnp.where(itself, own, MASKED))
                share = jnp.exp(jnp.minimum(scores, 0.0))
                grad_value = dot_nn(share.astype(BF16), grad)
                grad_scores = jnp.where(earlier, share * slope, 0.0).astype(BF16)
                grad_key = dot_nn(grad_scores, query)
                grad_query = dot_tn(grad_scores, key)
                along = jnp.sum(unit * grad_key, axis=1, keepdims=True)
                results.append((grad_query + inverse * (grad_key - unit * along), grad_value))
            for n in range(batch):
                left_ref[pl.ds(at[n], CAP, stride=plan.pitch), :] = results[n][0]
                right_ref[pl.ds(at[n], CAP, stride=plan.pitch), :] = results[n][1]
            return 0

        lax.fori_loop(0, plan.per_step // batch, some, 0)

    @pl.when(step >= first_scatter)
    def _():
        block = scal[2 + jnp.maximum(step - first_scatter, 0)]
        ranks_by_token(plan, named_ref, base, token_rank)
        block_rows(plan, left_ref, block, rhs_ref, slice(0, DH))
        block_rows(plan, right_ref, block, rhs_ref, slice(DH, 2 * DH))
        pairs = plan.most // 2

        def chunk(part, _):
            start = pl.multiple_of(part * plan.chunk, GROUP)
            for sub in range(plan.chunk // GROUP):
                rows = pl.ds(pl.multiple_of(start + sub * GROUP, GROUP), GROUP)
                here = slice(sub * GROUP, (sub + 1) * GROUP)
                for tile in range(plan.tiles):
                    ranks = token_rank[rows, tile * GROUP : (tile + 1) * GROUP]
                    for j in range(pairs):
                        to = (tile * pairs + j) * GROUP
                        lhs_ref[here, to : to + GROUP] = jnp.where(
                            ranks == pair_values(j), 1.0, 0.0
                        ).astype(BF16)
            found = dot_nn(lhs_ref[...], rhs_ref[...])
            shared_out[0, pl.ds(start, plan.chunk), :] = found[:, :DH].astype(BF16)
            value_out[0, pl.ds(start, plan.chunk), :] = found[:, DH:].astype(BF16)
            return 0

        lax.fori_loop(0, plan.tokens // plan.chunk, chunk, 0)


def backward_call(plan, scal, named, grads, slot_shared, slot_value):
    first_scatter = plan.blocks + plan.steps

    def named_at(i, scal):
        here = jnp.where(i < plan.blocks, i, jnp.maximum(i - first_scatter, 0))
        return (scal[2 + here], 0, 0)

    def table_at(i, scal):
        return (jnp.minimum(i, plan.blocks - 1), 0, 0)

    def slots_at(i, scal):
        return (jnp.clip(i - plan.blocks, 0, plan.steps - 1), 0, 0)

    def out_at(i, scal):
        return (jnp.maximum(i - first_scatter, 0), 0, 0)

    out = jax.ShapeDtypeStruct((plan.blocks, plan.tokens, DH), BF16)
    return pl.pallas_call(
        lambda *refs: backward_body(plan, *refs),
        grid_spec=pltpu.PrefetchScalarGridSpec(
            num_scalar_prefetch=1,
            grid=(plan.blocks + plan.steps + plan.blocks,),
            in_specs=[
                pl.BlockSpec((1, 8, plan.tokens), named_at),
                pl.BlockSpec((1, grads.shape[1], DH), table_at),
                pl.BlockSpec((plan.per_step, CAP, DH), slots_at),
                pl.BlockSpec((plan.per_step, CAP, DH), slots_at),
            ],
            out_specs=[
                pl.BlockSpec((1, plan.tokens, DH), out_at),
                pl.BlockSpec((1, plan.tokens, DH), out_at),
            ],
            scratch_shapes=[
                pltpu.VMEM((CAP * plan.pitch, DH), F32),
                pltpu.VMEM((CAP * plan.pitch, DH), F32),
                pltpu.VMEM((plan.rows, plan.tokens), F32),
                pltpu.VMEM((plan.tokens, plan.tiles * GROUP), F32),
                pltpu.VMEM((plan.tokens, GROUP), BF16),
                pltpu.VMEM((plan.chunk, plan.deep), BF16),
                pltpu.VMEM((plan.deep, 2 * DH), BF16),
            ],
        ),
        out_shape=[out, out],
        compiler_params=pltpu.CompilerParams(vmem_limit_bytes=VMEM_BYTES),
        name="bucket_backward",
    )(scal, named, grads, slot_shared, slot_value)


def norm_parts(row_block):
    row_mean = jnp.mean(row_block, axis=1, keepdims=True)
    centred = row_block - row_mean
    row_scale = lax.rsqrt(jnp.mean(centred * centred, axis=1, keepdims=True) + 1e-05)
    return centred * row_scale, row_scale


def norm_back(grad_norm, unit, row_scale, gain):
    grad_unit = grad_norm * gain
    first = jnp.mean(grad_unit, axis=1, keepdims=True)
    second = jnp.mean(grad_unit * unit, axis=1, keepdims=True)
    back = row_scale * (grad_unit - first - unit * second)
    return back, jnp.sum(grad_norm * unit, axis=0), jnp.sum(grad_norm, axis=0)


def smooth_gate(value_in):
    return jax.nn.gelu(value_in, approximate=True)


def head_swap(array_in, bits):
    return lax.ppermute(array_in, "head", [(i, i ^ bits) for i in range(4)])


def gather_features(shard):
    if lax.axis_size("head") != 4:
        return lax.all_gather(shard, "head", axis=1, tiled=True)
    half = shard.shape[0] // 2
    one, two = head_swap(shard, 1), head_swap(shard, 2)
    far = jnp.concatenate([head_swap(two[:half], 1), head_swap(one[half:], 2)], axis=0)
    me = lax.axis_index("head")
    by_distance = jnp.stack([shard, one, two, far])
    return jnp.concatenate(
        [lax.dynamic_index_in_dim(by_distance, me ^ n, 0, False) for n in range(4)], axis=1
    )


def sum_features(partial):
    devices = lax.axis_size("head")
    rows, width = partial.shape
    if devices != 4:
        return lax.psum_scatter(partial, "head", scatter_dimension=1, tiled=True).astype(F32)
    own = width // 4
    me = lax.axis_index("head")

    def piece(block, bits):
        return lax.dynamic_slice_in_dim(block, (me ^ bits) * own, own, 1)

    half = rows // 2
    sums = []
    for block, first, second in ((partial[:half], 1, 2), (partial[half:], 2, 1)):
        sent = jnp.concatenate([piece(block, first), piece(block, 3)], axis=1)
        got = head_swap(sent, first).astype(F32)
        passed = (piece(block, second).astype(F32) + got[:, own:]).astype(BF16)
        kept = piece(block, 0).astype(F32) + got[:, :own]
        sums.append(kept + head_swap(passed, second).astype(F32))
    return jnp.concatenate(sums, axis=0)


class Tokens:
    def __init__(self, heads_here):
        self.devices = lax.axis_size("tok")
        self.me = lax.axis_index("tok")
        self.heads = heads_here
        self.paired = self.devices == 8 and heads_here == 2
        self.group = self.devices // heads_here
        self.head = self.me // self.group
        self.quarter = self.me % self.group
        if self.paired:
            z, core = self.me // 2, self.me % 2
            chips = [z, 3 - z, z ^ 1, 3 - (z ^ 1)]
            self.order = jnp.stack(
                [c * 2 + core for c in chips] + [c * 2 + 1 - core for c in chips]
            )
        else:
            self.order = jnp.arange(self.devices)

    def swap(self, array_in, bits):
        return lax.ppermute(array_in, "tok", [(i, i ^ bits) for i in range(8)])

    def mirror(self, array_in):
        return lax.ppermute(array_in, "tok", [(i, 6 - 2 * (i // 2) + i % 2) for i in range(8)])

    def own_first(self, by_head):
        return jnp.where(self.head == 0, by_head, by_head[::-1])

    def spread(self, by_head):
        if self.paired:
            both = self.own_first(by_head)
            pair = jnp.stack([both[0], self.mirror(both[1])])
            four = jnp.concatenate([pair, self.swap(pair, 2)])
            return jnp.concatenate([four, self.swap(four, 1)])
        everyone = lax.all_gather(by_head, "tok", axis=0)
        return lax.dynamic_index_in_dim(everyone, self.head, 1, False)

    def collect(self, by_block, merge):
        if self.paired:
            four = merge([by_block[:4], self.swap(by_block[4:], 1)])
            pair = merge([four[:2], self.swap(four[2:], 2)])
            return self.own_first(jnp.stack([pair[0], self.mirror(pair[1])]))
        shares = lax.all_to_all(by_block, "tok", split_axis=0, concat_axis=0, tiled=True)
        shares = shares.reshape((self.heads, self.group) + shares.shape[1:])
        return merge([shares[:, n] for n in range(self.group)])


def add_up(parts):
    total = parts[0].astype(F32)
    for part in parts[1:]:
        total = total + part.astype(F32)
    return total.astype(BF16)


def by_head(columns):
    rows, width = columns.shape
    return jnp.stack([columns[:, n * DH : (n + 1) * DH] for n in range(width // DH)])


def to_columns(heads):
    return jnp.concatenate([heads[n] for n in range(heads.shape[0])], axis=1)


def shards(
    stream_one,
    stream_two,
    buckets,
    lengths,
    gain_attn,
    bias_attn,
    qk_weight,
    value_weight,
    out_weight,
    gain_ffn,
    bias_ffn,
    in_weight,
    in_bias,
    down_weight,
    down_bias,
    cotangent_one,
    cotangent_two,
):
    tok_rows, shard_width = stream_one.shape
    head_devices = lax.axis_size("head")
    tok_devices = lax.axis_size("tok")
    me_head, me_tok = lax.axis_index("head"), lax.axis_index("tok")
    full_width = shard_width * head_devices
    hidden_width = in_bias.shape[0]
    tokens = Tokens(shard_width // DH)
    per_device = 88
    plan = Plan(
        tok_devices, tok_rows, CAP // tok_devices, per_device * tok_devices // tokens.group
    )
    own = me_head * shard_width

    whole_qk = lax.all_gather(qk_weight, "tok", axis=0, tiled=True)
    whole_value = lax.all_gather(value_weight, "tok", axis=0, tiled=True)
    whole_out = lax.all_gather(
        lax.all_gather(out_weight, "tok", axis=1, tiled=True), "head", axis=0, tiled=True
    )
    whole_in = lax.all_gather(in_weight, "tok", axis=0, tiled=True)
    whole_down = lax.all_gather(down_weight, "tok", axis=1, tiled=True)
    vectors = lax.all_gather(
        jnp.stack([gain_attn, bias_attn, gain_ffn, bias_ffn]), "head", axis=1, tiled=True
    ).astype(F32)
    gain_one, bias_one, gain_two, bias_two = [vectors[n : n + 1] for n in range(4)]

    names = jnp.concatenate(
        [buckets.T.astype(F32), jnp.full((8 - buckets.shape[1], tok_rows), -5.0, F32)]
    )
    named = lax.all_gather(names, "tok", axis=0)
    scalars = jnp.concatenate(
        [jnp.stack([lengths[0], tokens.quarter * plan.buckets]), tokens.order]
    ).astype(jnp.int32)
    ids = (me_tok * per_device + jnp.arange(per_device)).astype(F32)
    bucket_counts = jnp.sum(
        (named[:, : buckets.shape[1]].reshape(1, -1) == ids[:, None]).astype(jnp.int32), axis=1
    )

    rows_two = gather_features(stream_two)
    unit_one, scale_one = norm_parts(rows_two.astype(F32))
    normed = (unit_one * gain_one + bias_one).astype(BF16)
    shared_tok = dot_nn(normed, whole_qk).astype(BF16)
    value_tok = dot_nn(normed, whole_value).astype(BF16)
    shared_all = tokens.spread(by_head(shared_tok))
    value_all = tokens.spread(by_head(value_tok))
    slot_shared, slot_value, shares = forward_call(plan, scalars, named, shared_all, value_all)
    mixed = tokens.collect(shares, merge_call)
    attended = gather_features(to_columns(mixed[:, :tok_rows]))

    rows_stream = gather_features(stream_one)
    rows_one = (rows_stream.astype(F32) + dot_nn(attended, whole_out)).astype(BF16)
    result_one = lax.dynamic_slice_in_dim(rows_one, own, shard_width, 1)
    unit_two, scale_two = norm_parts(rows_one.astype(F32))
    normed_two = (unit_two * gain_two + bias_two).astype(BF16)
    pre_act = dot_nn(normed_two, whole_in) + in_bias.astype(F32)
    hidden, gate_back = jax.vjp(smooth_gate, pre_act)
    hidden_low = hidden.astype(BF16)
    result_two = (
        stream_two.astype(F32)
        + sum_features(dot_nn(hidden_low, whole_down).astype(BF16))
        + down_bias.astype(F32)
    ).astype(BF16)
    rows_grad = gather_features(cotangent_two)
    grad_hidden = dot_nt(rows_grad, whole_down)
    grad_pre = gate_back(grad_hidden)[0].astype(BF16)
    back_two, gain_two_part, bias_two_part = norm_back(
        dot_nt(grad_pre, whole_in), unit_two, scale_two, gain_two
    )
    mine = (jnp.arange(full_width) // shard_width == me_head)[None, :]
    carried = (
        back_two + jnp.where(mine, jnp.tile(cotangent_one, (1, head_devices)).astype(F32), 0.0)
    ).astype(BF16)
    grad_attended = sum_features(dot_nt(carried, whole_out).astype(BF16)).astype(BF16)
    grad_one = sum_features(carried).astype(BF16)

    packed = pack_call(by_head(grad_attended), mixed)
    shared_part, value_part = backward_call(
        plan, scalars, named, tokens.spread(packed), slot_shared, slot_value
    )
    grad_shared = to_columns(tokens.collect(shared_part, add_up))
    grad_value = to_columns(tokens.collect(value_part, add_up))
    back_one, gain_one_part, bias_one_part = norm_back(
        dot_nt(grad_shared, whole_qk) + dot_nt(grad_value, whole_value),
        unit_one,
        scale_one,
        gain_one,
    )
    grad_two = (cotangent_two.astype(F32) + sum_features(back_one.astype(BF16))).astype(BF16)

    def over_tokens(part, axis):
        return lax.psum_scatter(
            part.astype(BF16), "tok", scatter_dimension=axis, tiled=True
        ).astype(F32)

    grad_down = over_tokens(dot_tn(hidden_low, rows_grad), 1)
    grad_in = over_tokens(dot_tn(normed_two, grad_pre), 0)
    out_part = dot_tn(attended, grad_one).astype(BF16)
    out_rows = lax.all_to_all(out_part, "head", split_axis=0, concat_axis=1, tiled=True)
    grad_out = over_tokens(out_rows, 1)
    grad_both = over_tokens(
        dot_tn(normed, jnp.concatenate([grad_shared, grad_value], axis=1)), 0
    )
    grad_qk, grad_v = grad_both[:, :shard_width], grad_both[:, shard_width:]

    def place(part):
        start = me_head * part.shape[0]
        whole = jnp.zeros((part.shape[0] * head_devices,), F32)
        return lax.dynamic_update_slice_in_dim(whole, part, start, 0)

    def share(whole):
        size = whole.shape[0] // (head_devices * tok_devices)
        return lax.dynamic_slice_in_dim(
            whole, (me_head * tok_devices + me_tok) * size, size, 0
        )

    early = lax.psum(
        jnp.concatenate(
            [
                gain_two_part,
                bias_two_part,
                place(jnp.sum(cotangent_two.astype(F32), axis=0)),
                place(jnp.sum(grad_pre.astype(F32), axis=0)),
            ]
        ),
        ("head", "tok"),
    )
    late = lax.psum(jnp.concatenate([gain_one_part, bias_one_part]), ("head", "tok"))
    return (
        result_one,
        result_two,
        grad_one,
        grad_two,
        share(late[:full_width]),
        share(late[full_width:]),
        grad_qk,
        grad_v,
        grad_out,
        share(early[:full_width]),
        share(early[full_width : 2 * full_width]),
        grad_in,
        share(early[3 * full_width :]),
        grad_down,
        share(early[2 * full_width : 3 * full_width]),
        bucket_counts,
    )


def solution(mesh):
    wide = P("tok", "head")
    placed = (
        wide, wide, P("tok", None), P(), P("head"), P("head"), wide, wide, P("head", "tok"),
        P("head"), P("head"), wide, P("head"), P("head", "tok"), P("head"), wide, wide,
    )
    vector = P(("head", "tok"))
    return jax.shard_map(
        shards,
        mesh=mesh,
        in_specs=placed,
        out_specs=(
            wide, wide, wide, wide, vector, vector, wide, wide, P("head", "tok"), vector, vector,
            wide, vector, P("head", "tok"), vector, P("tok"),
        ),
        check_vma=False,
    )
```

```python
import jax
import jax.numpy as jnp
from jax import lax
from jax.experimental import pallas as pl
from jax.experimental.pallas import tpu as pltpu
from jax.sharding import PartitionSpec as P

DH = 128
CAP = 128
GROUP = 128
ROWS = 256
TILE = 16
HALVES = 2

SELF_SCORE = -10000.0
MASKED = -1000000000.0
NOTHING = -1e30
LOWEST = -3e38
PENALTY = 1048576.0
F32 = jnp.float32
BF16 = jnp.bfloat16
VMEM_BYTES = 60 * 1024 * 1024


def round_up(value, multiple):
    return -(-value // multiple) * multiple


def iota(shape, axis):
    return lax.broadcasted_iota(jnp.int32, shape, axis)


def dot_nt(left, right):
    return lax.dot_general(left, right, (((1,), (1,)), ((), ())), preferred_element_type=F32)


def dot_tn(left, right):
    return lax.dot_general(left, right, (((0,), (0,)), ((), ())), preferred_element_type=F32)


def dot_nn(left, right):
    return jnp.dot(left, right, preferred_element_type=F32)


def split_three(value):
    high = value.astype(BF16).astype(F32)
    rest = value - high
    middle = rest.astype(BF16).astype(F32)
    return [high, middle, rest - middle]


def column_to_row(column):
    spread = jnp.broadcast_to(column, (GROUP, GROUP))
    same = iota((GROUP, GROUP), 0) == iota((GROUP, GROUP), 1)
    return jnp.sum(jnp.where(same, spread, 0.0), axis=0, keepdims=True)


NO_COST = pl.CostEstimate(flops=0, bytes_accessed=0, transcendentals=0)


def params():
    return pltpu.CompilerParams(vmem_limit_bytes=VMEM_BYTES)


class Plan:
    def __init__(self, blocks, tokens, most, buckets):
        self.blocks, self.tokens, self.most, self.buckets = blocks, tokens, most, buckets
        self.rows = round_up(buckets, TILE)
        self.steps = self.rows // TILE
        self.slots = self.rows * most
        self.half = tokens // HALVES
        self.groups = self.half // GROUP
        self.lse_rows = round_up(3 * self.groups, 16)
        self.dot_rows = round_up(2 * self.groups, 16)
        self.packed = self.half + self.lse_rows
        self.full = self.packed + self.dot_rows


def slot_order(plan, scal, axis):
    slot = iota((CAP, CAP), axis)
    order = jnp.zeros((CAP, CAP), F32)
    for n in range(plan.blocks):
        first = scal[1 + n] * plan.most - n * plan.most
        order = jnp.where(slot // plan.most == n, (slot + first).astype(F32), order)
    return order


def rank_call(plan, scal, named):
    def body(scal, named_ref, rank_ref, since_ref, empty_ref, code_ref):
        step = pl.program_id(0)
        boundary, base = scal[plan.blocks + 1], scal[0]
        block = scal[1 + step]
        row = iota((plan.rows, 1), 0)
        ids = jnp.where(row < plan.buckets, (row + base).astype(F32), -100.0)
        earlier = jnp.where(iota((ROWS, ROWS), 0) < iota((ROWS, ROWS), 1), 1.0, 0.0).astype(BF16)
        count = jnp.zeros((plan.rows, 1), F32)
        below = jnp.zeros((plan.rows, 1), F32)
        for part in range(plan.tokens // ROWS):
            cols = slice(part * ROWS, (part + 1) * ROWS)
            member = ids == named_ref[0, 0:1, cols]
            for r in range(1, 4):
                member = member | (ids == named_ref[0, r : r + 1, cols])
            ones = jnp.where(member, 1.0, 0.0)
            before = dot_nn(ones.astype(BF16), earlier)
            rank_ref[0, :, cols] = jnp.where(member, before + count, -1.0).astype(BF16)
            place = block * plan.tokens + part * ROWS + iota((1, ROWS), 1)
            below = below + jnp.sum(jnp.where(place < boundary, ones, 0.0), axis=1, keepdims=True)
            count = count + jnp.sum(ones, axis=1, keepdims=True)

        @pl.when(step == 0)
        def _():
            code_ref[...] = jnp.zeros_like(code_ref)

        nth = iota((plan.rows, CAP), 1) - step * plan.most
        valid = (nth >= 0) & (nth < plan.most) & (nth.astype(F32) < count)
        code_ref[...] = jnp.where(
            valid, jnp.where(nth.astype(F32) < below, 1.0, 2.0), code_ref[...]
        )

        @pl.when(step == plan.blocks - 1)
        def _():
            code = code_ref[...]
            order = slot_order(plan, scal, 1)[0:1, :]
            change = jnp.min(jnp.where(code == 2.0, order, 1.0 * CAP), axis=1, keepdims=True)
            since_ref[...] = jnp.where(order >= change, change, 0.0)
            empty = jnp.where(code == 0.0, -PENALTY, 0.0)
            pad = round_up(plan.rows, GROUP) - plan.rows
            if pad:
                empty = jnp.concatenate([empty, jnp.zeros((pad, CAP), F32)], axis=0)
            for n in range(empty.shape[0] // GROUP):
                empty_ref[n] = jnp.transpose(empty[n * GROUP : (n + 1) * GROUP]).astype(BF16)

    sets = -(-plan.rows // GROUP)
    return pl.pallas_call(
        body,
        grid_spec=pltpu.PrefetchScalarGridSpec(
            num_scalar_prefetch=1,
            grid=(plan.blocks,),
            in_specs=[pl.BlockSpec((1, 8, plan.tokens), lambda i, scal: (i, 0, 0))],
            out_specs=[
                pl.BlockSpec((1, plan.rows, plan.tokens), lambda i, scal: (i, 0, 0)),
                pl.BlockSpec((plan.rows, CAP), lambda i, scal: (0, 0)),
                pl.BlockSpec((sets, CAP, GROUP), lambda i, scal: (0, 0, 0)),
            ],
            scratch_shapes=[pltpu.VMEM((plan.rows, CAP), F32)],
        ),
        out_shape=[
            jax.ShapeDtypeStruct((plan.blocks, plan.rows, plan.tokens), BF16),
            jax.ShapeDtypeStruct((plan.rows, CAP), F32),
            jax.ShapeDtypeStruct((sets, CAP, GROUP), BF16),
        ],
        compiler_params=params(),
        cost_estimate=NO_COST,
        name="bucket_ranks",
    )(scal, named)


def spread_rows(plan, rows):
    return jnp.concatenate(
        [
            jnp.broadcast_to(rows[n : n + 1], (plan.most, rows.shape[1]))
            for n in range(rows.shape[0])
        ],
        axis=0,
    )


def gather_rows(plan, rank_ref, table, more):
    number = (iota((plan.slots, ROWS), 0) % plan.most).astype(F32)
    picks = []
    for part in range(plan.half // ROWS):
        cols = slice(part * ROWS, (part + 1) * ROWS)
        ranks = spread_rows(plan, rank_ref[0, :, cols].astype(F32))
        picks.append(jnp.where(ranks == number, 1.0, 0.0).astype(BF16))
    found = dot_nn(jnp.concatenate(picks, axis=1), table)
    for ref in more:
        found = found + ref[0].astype(F32)
    return found.astype(BF16)


def rank_spec(plan, first, half):
    return pl.BlockSpec((1, plan.rows, plan.half), lambda i, *_: (i + first, 0, half))


def slot_spec(plan, width, first=0):
    return pl.BlockSpec((1, plan.slots, width), lambda i, *_: (i + first, 0, 0))


def gather_call(plan, ranks, rows, first, half, more):
    count = rows.shape[0]

    def body(rank_ref, rows_ref, *refs):
        refs[-1][0] = gather_rows(plan, rank_ref, rows_ref[0], refs[:-1])

    return pl.pallas_call(
        body,
        grid=(count,),
        in_specs=[
            rank_spec(plan, first, half),
            pl.BlockSpec((1, plan.half, 2 * DH), lambda i: (i, 0, 0)),
        ]
        + [slot_spec(plan, 2 * DH)] * len(more),
        out_specs=slot_spec(plan, 2 * DH),
        out_shape=jax.ShapeDtypeStruct((count, plan.slots, 2 * DH), BF16),
        compiler_params=params(),
        cost_estimate=NO_COST,
        name="gather_slots",
    )(ranks, rows, *more)


def gather_back_call(plan, scal, ranks, packed, first, half, more):
    count = packed.shape[0]

    def body(scal, rank_ref, ref, *refs):
        block = scal[1 + first + pl.program_id(0)]
        boundary = scal[plan.blocks + 1]
        lane = iota((1, GROUP), 1)
        spread = jnp.where(iota((8, GROUP), 0) == iota((8, GROUP), 1), 1.0, 0.0).astype(BF16)
        small = ref[0, plan.half : plan.full, :].astype(F32)
        extras = []
        for g in range(plan.groups):
            place = block * plan.tokens + half * plan.half + g * GROUP + lane
            rows = [small[n * plan.groups + g : n * plan.groups + g + 1, :] for n in range(3)]
            for n in range(2):
                at = plan.lse_rows + n * plan.groups + g
                rows.append(small[at : at + 1, :])
            rows.append(jnp.where(place < boundary, 1.0, 0.0))
            rows.append(jnp.zeros((2, GROUP), F32))
            extras.append(dot_tn(jnp.concatenate(rows, axis=0).astype(BF16), spread).astype(BF16))
        table = jnp.concatenate(
            [ref[0, : plan.half, :], jnp.concatenate(extras, axis=0)], axis=1
        )
        refs[-1][0] = gather_rows(plan, rank_ref, table, refs[:-1])

    return pl.pallas_call(
        body,
        grid_spec=pltpu.PrefetchScalarGridSpec(
            num_scalar_prefetch=1,
            grid=(count,),
            in_specs=[
                rank_spec(plan, first, half),
                pl.BlockSpec((1, plan.full, DH), lambda i, scal: (i, 0, 0)),
            ]
            + [slot_spec(plan, 2 * DH)] * len(more),
            out_specs=slot_spec(plan, 2 * DH),
        ),
        out_shape=jax.ShapeDtypeStruct((count, plan.slots, 2 * DH), BF16),
        compiler_params=params(),
        cost_estimate=NO_COST,
        name="gather_gradient",
    )(scal, ranks, packed, *more)


def table_of(plan, refs, bucket):
    rows = slice(bucket * plan.most, (bucket + 1) * plan.most)
    return jnp.concatenate([ref[n, rows, :] for ref in refs for n in range(ref.shape[0])], axis=0)


def tile_specs(plan, arrays):
    return [
        pl.BlockSpec((a.shape[0], TILE * plan.most, a.shape[2]), lambda i, scal: (0, i, 0))
        for a in arrays
    ]


def attention_call(plan, scal, slots, since, empty):
    count = len(slots)

    def body(scal, *refs):
        ins, since_ref, empty_ref = refs[:count], refs[count], refs[count + 1]
        out_ref, total_ref, key_order, query_order = refs[count + 2 :]
        step = pl.program_id(0)

        @pl.when(step == 0)
        def _():
            key_order[...] = slot_order(plan, scal, 0)
            query_order[...] = slot_order(plan, scal, 1)

        lane = iota((1, GROUP), 1)
        per = GROUP // TILE
        own = iota((CAP, CAP), 0) == iota((CAP, CAP), 1)
        for b in range(TILE):
            both = table_of(plan, ins, b)
            query, value = both[:, :DH], both[:, DH:]
            wide = query.astype(F32)
            inverse = lax.rsqrt(jnp.sum(wide * wide, axis=1, keepdims=True) + 1e-06)
            key = (wide * inverse).astype(BF16)
            mine = jnp.where(lane == lax.rem(step, per) * TILE + b, 1.0, 0.0)
            scores = dot_nt(
                jnp.concatenate([key, empty_ref[step // per]], axis=1),
                jnp.concatenate(
                    [query, jnp.broadcast_to(mine, (CAP, GROUP)).astype(BF16)], axis=1
                ),
            )
            allowed = (key_order[...] < query_order[...]) & (
                key_order[...] >= since_ref[b : b + 1, :]
            )
            scores = jnp.where(allowed, scores, jnp.where(own, SELF_SCORE, MASKED))
            highest = jnp.max(scores, axis=0, keepdims=True)
            raised = jnp.exp(scores - highest)
            summed = jnp.sum(raised, axis=0, keepdims=True)
            weight = (raised * (1.0 / summed)).astype(BF16)
            mixture = dot_tn(weight, value).astype(BF16)
            for n in range(plan.blocks):
                out_ref[n, b * plan.most : (b + 1) * plan.most, :] = mixture[
                    n * plan.most : (n + 1) * plan.most
                ]
            total_ref[b : b + 1, :] = highest + jnp.log(summed)

    return pl.pallas_call(
        body,
        grid_spec=pltpu.PrefetchScalarGridSpec(
            num_scalar_prefetch=1,
            grid=(plan.steps,),
            in_specs=tile_specs(plan, slots)
            + [
                pl.BlockSpec((TILE, CAP), lambda i, scal: (i, 0)),
                pl.BlockSpec(empty.shape, lambda i, scal: (0, 0, 0)),
            ],
            out_specs=[
                pl.BlockSpec((plan.blocks, TILE * plan.most, DH), lambda i, scal: (0, i, 0)),
                pl.BlockSpec((TILE, CAP), lambda i, scal: (i, 0)),
            ],
            scratch_shapes=[pltpu.VMEM((CAP, CAP), F32), pltpu.VMEM((CAP, CAP), F32)],
        ),
        out_shape=[
            jax.ShapeDtypeStruct((plan.blocks, plan.slots, DH), BF16),
            jax.ShapeDtypeStruct((plan.rows, CAP), F32),
        ],
        compiler_params=params(),
        cost_estimate=NO_COST,
        name="bucket_attention",
    )(scal, *slots, since, empty)


def attention_back_call(plan, scal, slots, grads):
    count = len(slots)

    def body(scal, *refs):
        ins, grad_ins = refs[:count], refs[count : 2 * count]
        out_ref, key_order, query_order = refs[2 * count :]

        @pl.when(pl.program_id(0) == 0)
        def _():
            key_order[...] = slot_order(plan, scal, 0)
            query_order[...] = slot_order(plan, scal, 1)

        lane = iota((1, GROUP), 1)
        itself = iota((CAP, CAP), 0) == iota((CAP, CAP), 1)
        query_scale = jnp.where(lane == 5, PENALTY, 1.0)
        query_shift = jnp.where(lane == 5, -PENALTY, 0.0)
        key_scale = jnp.where(lane == 5, 1.0, 0.0)
        key_shift = jnp.where(lane < 3, -1.0, 0.0)
        value_extra = jnp.broadcast_to(
            jnp.where((lane == 3) | (lane == 4), -1.0, 0.0), (CAP, GROUP)
        ).astype(BF16)
        minus_total = jnp.broadcast_to(key_shift, (16, GROUP)).astype(BF16)
        for b in range(TILE):
            both, grad_extra = table_of(plan, ins, b), table_of(plan, grad_ins, b)
            query, value = both[:, :DH], both[:, DH:]
            grad, extra = grad_extra[:, :DH], grad_extra[:, DH:]
            wide = query.astype(F32)
            inverse = lax.rsqrt(jnp.sum(wide * wide, axis=1, keepdims=True) + 1e-06)
            unit = wide * inverse
            key = unit.astype(BF16)
            extra_wide = extra.astype(F32)
            query_extra = (extra_wide * query_scale + query_shift).astype(BF16)
            key_extra = (extra_wide * key_scale + key_shift).astype(BF16)
            scores = dot_nt(
                jnp.concatenate([key, key_extra], axis=1),
                jnp.concatenate([query, query_extra], axis=1),
            )
            slope = dot_nt(jnp.concatenate([value, value_extra], axis=1), grad_extra)
            own = dot_nt(minus_total, extra)[0:1, :] + SELF_SCORE
            earlier = key_order[...] < query_order[...]
            scores = jnp.where(earlier, scores, jnp.where(itself, own, MASKED))
            share = jnp.exp(jnp.minimum(scores, 0.0))
            grad_value = dot_nn(share.astype(BF16), grad)
            grad_scores = jnp.where(earlier, share * slope, 0.0).astype(BF16)
            grad_key = dot_nn(grad_scores, query)
            grad_query = dot_tn(grad_scores, key)
            along = jnp.sum(unit * grad_key, axis=1, keepdims=True)
            grad_shared = (grad_query + inverse * (grad_key - unit * along)).astype(BF16)
            grad_value = grad_value.astype(BF16)
            for n in range(plan.blocks):
                to = slice(b * plan.most, (b + 1) * plan.most)
                rows = slice(n * plan.most, (n + 1) * plan.most)
                out_ref[n, to, :DH] = grad_shared[rows]
                out_ref[n, to, DH:] = grad_value[rows]

    return pl.pallas_call(
        body,
        grid_spec=pltpu.PrefetchScalarGridSpec(
            num_scalar_prefetch=1,
            grid=(plan.steps,),
            in_specs=tile_specs(plan, slots) + tile_specs(plan, grads),
            out_specs=pl.BlockSpec(
                (plan.blocks, TILE * plan.most, 2 * DH), lambda i, scal: (0, i, 0)
            ),
            scratch_shapes=[pltpu.VMEM((CAP, CAP), F32), pltpu.VMEM((CAP, CAP), F32)],
        ),
        out_shape=jax.ShapeDtypeStruct((plan.blocks, plan.slots, 2 * DH), BF16),
        compiler_params=params(),
        cost_estimate=NO_COST,
        name="bucket_attention_back",
    )(scal, *slots, *grads)


def columns_of(plan, slot_ref):
    return jnp.transpose(slot_ref[0].astype(F32)).astype(BF16)


def scatter_rows(plan, rank_ref, weight_ref, columns):
    number = (iota((TILE * plan.most, plan.half), 0) % plan.most).astype(F32)
    found = []
    for n in range(plan.steps):
        buckets = slice(n * TILE, (n + 1) * TILE)
        hit = spread_rows(plan, rank_ref[0, buckets, :].astype(F32)) == number
        weight = 1.0 if weight_ref is None else spread_rows(plan, weight_ref[buckets, :])
        found.append(jnp.where(hit, weight, 0.0).astype(BF16))
    return dot_nn(columns, jnp.concatenate(found, axis=0))


def scatter_call(plan, ranks, results, totals, first, count, half):
    def body(rank_ref, result_ref, total_ref, out_ref, found_ref, top_ref, lse_ref):
        first_slot = (first + pl.program_id(0)) * plan.most

        def totals_here(turn, tops):
            rows = pl.ds(pl.multiple_of(turn * 16, 16), 16)
            mine = total_ref[rows, :]
            new = []
            for g in range(plan.groups):
                cols = slice(g * GROUP, (g + 1) * GROUP)
                rank = rank_ref[0, rows, cols].astype(F32)
                at = jnp.maximum(rank, 0.0).astype(jnp.int32) + first_slot
                top = tops[g]
                for n in range(2):
                    part = slice(n * 8, (n + 1) * 8)
                    found = jnp.where(
                        rank[part] >= 0.0,
                        jnp.take_along_axis(mine[part], at[part], axis=1),
                        LOWEST,
                    )
                    found_ref[pl.ds(pl.multiple_of(turn * 16 + n * 8, 8), 8), cols] = found
                    top = jnp.maximum(top, found)
                new.append(top)
            return tuple(new)

        tops = lax.fori_loop(
            0,
            plan.rows // 16,
            totals_here,
            tuple(jnp.full((8, GROUP), LOWEST, F32) for _ in range(plan.groups)),
        )
        for g in range(plan.groups):
            top_ref[g] = tops[g]

        def weights(g, _):
            cols = pl.ds(pl.multiple_of(g * GROUP, GROUP), GROUP)
            top = jnp.max(top_ref[g], axis=0, keepdims=True)
            weight = jnp.exp(found_ref[:, cols] - jnp.where(top > 0.1 * LOWEST, top, 0.0))
            summed = jnp.sum(weight, axis=0, keepdims=True)
            some_here = summed > 0.0
            safe = jnp.where(some_here, summed, 1.0)
            found_ref[:, cols] = weight * (1.0 / safe)
            lse_ref[pl.ds(g, 1), :] = jnp.where(some_here, top + jnp.log(safe), NOTHING)
            return 0

        lax.fori_loop(0, plan.groups, weights, 0)
        found = scatter_rows(plan, rank_ref, found_ref, columns_of(plan, result_ref))
        out_ref[0, : plan.half, :] = jnp.transpose(found).astype(BF16)
        pieces = split_three(lse_ref[...])
        rest = plan.lse_rows - 3 * plan.groups
        if rest:
            pieces.append(jnp.zeros((rest, GROUP), F32))
        out_ref[0, plan.half :, :] = jnp.concatenate(pieces, axis=0).astype(BF16)

    return pl.pallas_call(
        body,
        grid=(count,),
        in_specs=[
            rank_spec(plan, first, half),
            slot_spec(plan, DH, first),
            pl.BlockSpec((plan.rows, CAP), lambda i: (0, 0)),
        ],
        out_specs=pl.BlockSpec((1, plan.packed, DH), lambda i: (i, 0, 0)),
        out_shape=jax.ShapeDtypeStruct((count, plan.packed, DH), BF16),
        scratch_shapes=[
            pltpu.VMEM((plan.rows, plan.half), F32),
            pltpu.VMEM((plan.groups, 8, GROUP), F32),
            pltpu.VMEM((plan.groups, GROUP), F32),
        ],
        compiler_params=params(),
        cost_estimate=NO_COST,
        name="scatter_results",
    )(ranks, results, totals)


def scatter_back_call(plan, ranks, grads, first, count, half):
    def body(rank_ref, grad_ref, out_ref):
        found = scatter_rows(plan, rank_ref, None, columns_of(plan, grad_ref))
        out_ref[0] = jnp.transpose(found).astype(BF16)

    return pl.pallas_call(
        body,
        grid=(count,),
        in_specs=[rank_spec(plan, first, half), slot_spec(plan, 2 * DH, first)],
        out_specs=pl.BlockSpec((1, plan.half, 2 * DH), lambda i: (i, 0, 0)),
        out_shape=jax.ShapeDtypeStruct((count, plan.half, 2 * DH), BF16),
        compiler_params=params(),
        cost_estimate=NO_COST,
        name="scatter_gradient",
    )(ranks, grads)


def merge_call(plan, parts):
    count = parts[0].shape[0]

    def body(*refs):
        ins, out_ref = refs[:-1], refs[-1]
        lses = []
        for ref in ins:
            small = ref[0, plan.half :, :].astype(F32)
            lses.append(
                sum(small[n * plan.groups : (n + 1) * plan.groups, :] for n in range(3))
            )
        highest = lses[0]
        for lse in lses[1:]:
            highest = jnp.maximum(highest, lse)
        raised = [jnp.exp(lse - highest) for lse in lses]
        summed = sum(raised)
        shares = [one / summed for one in raised]
        pieces = split_three(highest + jnp.log(summed))
        rest = plan.lse_rows - 3 * plan.groups
        if rest:
            pieces.append(jnp.zeros((rest, GROUP), F32))
        out_ref[0, plan.half :, :] = jnp.concatenate(pieces, axis=0).astype(BF16)
        low = [piece for share in shares for piece in split_three(share)[:2]]
        ones = [
            jnp.where(iota((8, GROUP), 0) // 2 == n, 1.0, 0.0).astype(BF16) for n in range(4)
        ]
        for g in range(plan.groups):
            rows = slice(g * GROUP, (g + 1) * GROUP)
            total = jnp.zeros((GROUP, DH), F32)
            for first in range(0, len(ins), 4):
                some = low[2 * first : 2 * first + 8]
                lines = [piece[g : g + 1, :] for piece in some]
                if len(lines) < 8:
                    lines.append(jnp.zeros((8 - len(lines), GROUP), F32))
                stack = jnp.concatenate(lines, axis=0).astype(BF16)
                for n, ref in enumerate(ins[first : first + 4]):
                    total = total + dot_tn(stack, ones[n]) * ref[0, rows, :].astype(F32)
            out_ref[0, rows, :] = total.astype(BF16)

    spec = pl.BlockSpec((1, plan.packed, DH), lambda i: (i, 0, 0))
    return pl.pallas_call(
        body,
        grid=(count,),
        in_specs=[spec] * len(parts),
        out_specs=spec,
        out_shape=jax.ShapeDtypeStruct((count, plan.packed, DH), BF16),
        compiler_params=params(),
        cost_estimate=NO_COST,
        name="merge_rounds",
    )(*parts)


def pack_call(plan, grads, mixed):
    heads = len(mixed)
    terms = [len(parts) for parts in grads]
    flat = [array for parts in grads for array in parts]

    def body(*refs):
        ins, mixed_refs, outs = refs[: len(flat)], refs[len(flat) : -heads], refs[-heads:]
        at = 0
        for n in range(heads):
            grad = ins[at][...].astype(F32)
            for ref in ins[at + 1 : at + terms[n]]:
                grad = grad + ref[...].astype(F32)
            at += terms[n]
            low = grad.astype(BF16)
            outs[n][: plan.half, :] = low
            outs[n][plan.half : plan.packed, :] = mixed_refs[n][plan.half :, :]
            wide = low.astype(F32)
            rows = []
            for g in range(plan.groups):
                here = slice(g * GROUP, (g + 1) * GROUP)
                product = wide[here] * mixed_refs[n][here, :].astype(F32)
                rows.append(column_to_row(jnp.sum(product, axis=1, keepdims=True)))
            dots = jnp.concatenate(rows, axis=0)
            high = dots.astype(BF16).astype(F32)
            pieces = [high, dots - high]
            rest = plan.dot_rows - 2 * plan.groups
            if rest:
                pieces.append(jnp.zeros((rest, GROUP), F32))
            outs[n][plan.packed :, :] = jnp.concatenate(pieces, axis=0).astype(BF16)

    return pl.pallas_call(
        body,
        out_shape=[jax.ShapeDtypeStruct((plan.full, DH), BF16)] * heads,
        compiler_params=params(),
        cost_estimate=NO_COST,
        name="pack_gradient",
    )(*flat, *mixed)


def unit_rows(wide):
    mean = jnp.mean(wide, axis=1, keepdims=True)
    centred = wide - mean
    scale = lax.rsqrt(jnp.mean(centred * centred, axis=1, keepdims=True) + 1e-05)
    return centred * scale, scale


def norm_back(grad_norm, unit, scale, gain):
    grad_unit = grad_norm * gain
    first = jnp.mean(grad_unit, axis=1, keepdims=True)
    second = jnp.mean(grad_unit * unit, axis=1, keepdims=True)
    return scale * (grad_unit - first - unit * second)


def row_spec(array, first=0):
    return pl.BlockSpec((ROWS, array.shape[1]), lambda i, *_: (i + first, 0))


def whole_spec(array):
    return pl.BlockSpec(array.shape, lambda i, *_: (0, 0))


def in_order(me, refs):
    if len(refs) == 1:
        return refs[0][...]
    parts = [ref[...] for ref in refs]
    columns = []
    for n in range(len(parts)):
        column = parts[n]
        for m in range(1, len(parts)):
            column = jnp.where(me == m, parts[n ^ m], column)
        columns.append(column)
    return jnp.concatenate(columns, axis=1)


def own_columns(me, array, width):
    mine = array[:, :width]
    for n in range(1, array.shape[1] // width):
        mine = jnp.where(me == n, array[:, n * width : (n + 1) * width], mine)
    return mine


def share_shapes(rows, width, devices):
    if devices != 4:
        return [jax.ShapeDtypeStruct((rows, width), BF16)]
    return [jax.ShapeDtypeStruct((rows, width // 2), BF16)] * 2


def put_share(me, early, refs, share):
    if len(refs) == 1:
        refs[0][...] = share.astype(BF16)
        return
    width = share.shape[1] // 4
    columns = [share[:, n * width : (n + 1) * width].astype(BF16) for n in range(4)]
    at = []
    for distance in range(4):
        column = columns[distance]
        for m in range(1, 4):
            column = jnp.where(me == m, columns[m ^ distance], column)
        at.append(column)
    sent, kept = refs
    sent[:, :width] = jnp.where(early, at[1], at[2])
    sent[:, width:] = at[3]
    kept[:, :width] = at[0]
    kept[:, width:] = jnp.where(early, at[2], at[1])


def norm_call(places, pieces, vectors, weight, heads):
    count = len(pieces)
    rows, width = pieces[0].shape[0], weight.shape[0]
    each = weight.shape[1] // heads

    def body(places, *refs):
        vectors_ref, weight_ref, rows_ref, normed_ref = refs[count : count + 4]
        outs = refs[count + 4 :]
        whole = in_order(places[0], refs[:count])
        rows_ref[...] = whole
        unit, _ = unit_rows(whole.astype(F32))
        normed = (unit * vectors_ref[0:1, :] + vectors_ref[1:2, :]).astype(BF16)
        normed_ref[...] = normed
        both = dot_nn(normed, weight_ref[...]).astype(BF16)
        parts = [both[:, n * each : (n + 1) * each] for n in range(heads)]
        if heads == 2:
            parts = [jnp.where(places[1] == n, parts[1], parts[0]) for n in (1, 0)]
        for out, part in zip(outs, parts):
            out[...] = part

    outs = [jax.ShapeDtypeStruct((rows, width), BF16)] * 2
    outs += [jax.ShapeDtypeStruct((rows, each), BF16)] * heads
    return pl.pallas_call(
        body,
        grid_spec=pltpu.PrefetchScalarGridSpec(
            num_scalar_prefetch=1,
            grid=(rows // ROWS,),
            in_specs=[row_spec(p) for p in pieces] + [whole_spec(vectors), whole_spec(weight)],
            out_specs=[row_spec(o) for o in outs],
        ),
        out_shape=outs,
        compiler_params=params(),
        cost_estimate=NO_COST,
        name="norm_project",
    )(places, *pieces, vectors, weight)


def norm_back_call(places, devices, rows, vectors, weight, grads):
    heads = len(grads)
    each = weight.shape[1] // heads

    def body(places, rows_ref, vectors_ref, weight_ref, *refs):
        outs, sums_ref = refs[heads:-1], refs[-1]
        unit, scale = unit_rows(rows_ref[...].astype(F32))
        parts = [ref[...] for ref in refs[:heads]]
        if heads == 2:
            parts = [jnp.where(places[1] == n, parts[1], parts[0]) for n in (1, 0)]
        grad = dot_nt(jnp.concatenate(parts, axis=1), weight_ref[...])
        back = norm_back(grad, unit, scale, vectors_ref[0:1, :])
        step = pl.program_id(0)
        early = pl.program_id(0) < pl.num_programs(0) // 2
        put_share(places[0], early, outs, back)

        @pl.when(step == 0)
        def _():
            sums_ref[...] = jnp.zeros_like(sums_ref)

        sums_ref[0:1, :] += jnp.sum(grad * unit, axis=0, keepdims=True)
        sums_ref[1:2, :] += jnp.sum(grad, axis=0, keepdims=True)

    outs = share_shapes(*rows.shape, devices)
    sums = jax.ShapeDtypeStruct((8, rows.shape[1]), F32)
    return pl.pallas_call(
        body,
        grid_spec=pltpu.PrefetchScalarGridSpec(
            num_scalar_prefetch=1,
            grid=(rows.shape[0] // ROWS,),
            in_specs=[row_spec(rows), whole_spec(vectors), whole_spec(weight)]
            + [row_spec(g) for g in grads],
            out_specs=[row_spec(o) for o in outs] + [whole_spec(sums)],
        ),
        out_shape=outs + [sums],
        compiler_params=params(),
        cost_estimate=NO_COST,
        name="norm_project_back",
    )(places, rows, vectors, weight, *grads)


CURVE = 0.7978845608028654
CUBIC = 0.044715


def feed_forward_call(
    places, devices, half, stream, pieces, grads, cotangent, vectors, in_bias, out_cols, in_weight,
    down_cols, before,
):
    own = cotangent.shape[1]
    count = len(pieces)
    rows, width = pieces[0].shape[0], stream.shape[1]
    deep = in_bias.shape[1]
    attended_width = out_cols.shape[1]
    widths = (attended_width, own, width, deep, deep, width, width)

    def body(places, *refs):
        piece_refs = refs[:count]
        stream_ref, grad_ref, cot_ref, vectors_ref, bias_ref, out_w, in_w, down_w = refs[
            count : count + 8
        ]
        (
            attended_ref, first_ref, normed_ref, hidden_ref, pre_ref, carried_ref, second_ref,
            sums_ref, hidden_sums,
        ) = refs[count + 8 + len(before) : count + 17 + len(before)]
        shares = refs[count + 17 + len(before) :]
        me = places[0]
        step = pl.program_id(0)
        attended = in_order(me, piece_refs)
        attended_ref[...] = attended
        result = (stream_ref[...].astype(F32) + dot_nt(attended, out_w[...])).astype(BF16)
        first_ref[...] = own_columns(me, result, own)
        unit, scale = unit_rows(result.astype(F32))
        normed = (unit * vectors_ref[2:3, :] + vectors_ref[3:4, :]).astype(BF16)
        normed_ref[...] = normed
        pre = dot_nn(normed, in_w[...]) + bias_ref[...]
        square = pre * pre
        bent = jnp.tanh(CURVE * (pre + CUBIC * square * pre))
        hidden = (0.5 * pre * (1.0 + bent)).astype(BF16)
        hidden_ref[...] = hidden
        slope = 0.5 * (1.0 + bent) + 0.5 * pre * (1.0 - bent * bent) * (
            CURVE * (1.0 + 3.0 * CUBIC * square)
        )
        grad_pre = (dot_nn(grad_ref[...], down_w[...]) * slope).astype(BF16)
        pre_ref[...] = grad_pre
        grad_norm = dot_nt(grad_pre, in_w[...])
        back = norm_back(grad_norm, unit, scale, vectors_ref[2:3, :])
        carried = jnp.concatenate(
            [
                back[:, n * own : (n + 1) * own]
                + jnp.where(me == n, cot_ref[...].astype(F32), 0.0)
                for n in range(width // own)
            ],
            axis=1,
        ).astype(BF16)
        carried_ref[...] = carried
        early = step < pl.num_programs(0) // 2
        put_share(me, early, shares, dot_nn(carried, out_w[...]))
        second_ref[...] = dot_nt(hidden, down_w[...]).astype(BF16)

        @pl.when(step == 0)
        def _():
            sums_ref[...] = jnp.zeros_like(sums_ref)
            hidden_sums[...] = jnp.zeros_like(hidden_sums)

        sums_ref[0:1, :] += jnp.sum(grad_norm * unit, axis=0, keepdims=True)
        sums_ref[1:2, :] += jnp.sum(grad_norm, axis=0, keepdims=True)
        hidden_sums[0:1, :] += jnp.sum(grad_pre.astype(F32), axis=0, keepdims=True)

    outs = [jax.ShapeDtypeStruct((stream.shape[0], w), BF16) for w in widths]
    sums = [jax.ShapeDtypeStruct((8, w), F32) for w in (width, deep)]
    shares = share_shapes(rows, attended_width, devices)
    first = half * (rows // ROWS)
    return pl.pallas_call(
        body,
        grid_spec=pltpu.PrefetchScalarGridSpec(
            num_scalar_prefetch=1,
            grid=(rows // ROWS,),
            in_specs=[row_spec(p) for p in pieces]
            + [row_spec(a, first) for a in (stream, grads, cotangent)]
            + [whole_spec(a) for a in (vectors, in_bias, out_cols)]
            + [pl.BlockSpec((width, deep), lambda i, *_: (0, 0))] * 2
            + [pl.BlockSpec(memory_space=pl.ANY)] * len(before),
            out_specs=[row_spec(o, first) for o in outs]
            + [whole_spec(o) for o in sums]
            + [row_spec(o) for o in shares],
        ),
        out_shape=outs + sums + shares,
        input_output_aliases={count + 9 + n: n for n in range(len(before))},
        compiler_params=params(),
        cost_estimate=NO_COST,
        name="feed_forward",
    )(
        places, *pieces, stream, grads, cotangent, vectors, in_bias, out_cols, in_weight, down_cols,
        *before,
    )


class Order:
    def __init__(self):
        self.last = None

    def tie(self, *arrays):
        if self.last is not None:
            arrays = lax.optimization_barrier((*arrays, self.last))[:-1]
        return arrays if len(arrays) > 1 else arrays[0]

    def mark(self, *arrays):
        self.last = arrays[0]
        return arrays if len(arrays) > 1 else arrays[0]


class Steps:
    def __init__(self, steps):
        self.steps = steps
        self.result = None

    def go(self, count=1):
        for _ in range(count):
            got = next(self.steps, None)
            self.result = self.result if got is None else got
        return self.result


def head_swap(array_in, bits):
    return lax.ppermute(array_in, "head", [(i, i ^ bits) for i in range(4)])


def gather_features(order, shard, direct=False):
    shard = order.tie(shard)
    if lax.axis_size("head") != 4:
        whole = [lax.all_gather(shard, "head", axis=1, tiled=True)]
        yield whole
        yield whole
        return
    one, two = head_swap(shard, 1), head_swap(shard, 2)
    if direct:
        far = head_swap(shard, 3)
        yield
        yield [shard, one, two, far]
        return
    yield
    half = round_up(shard.shape[0] // 2, 16)
    one, two = order.mark(*order.tie(one, two))
    far = jnp.concatenate([head_swap(two[:half], 1), head_swap(one[half:], 2)], axis=0)
    yield [shard, one, two, far]


def sum_terms(order, share):
    if len(share) == 1:
        share = order.tie(share[0])
        whole = [lax.psum_scatter(share, "head", scatter_dimension=1, tiled=True)]
        yield whole
        yield whole
        return
    sent, kept = order.tie(*share)
    half, own = sent.shape[0] // 2, sent.shape[1] // 2
    low, high = head_swap(sent[:half], 1), head_swap(sent[half:], 2)
    yield
    low, high = order.mark(*order.tie(low, high))
    passed = [
        (mine.astype(F32) + other.astype(F32)).astype(BF16)
        for mine, other in ((kept[:half, own:], low[:, own:]), (kept[half:, own:], high[:, own:]))
    ]
    last = jnp.concatenate([head_swap(passed[0], 2), head_swap(passed[1], 1)])
    yield [kept[:, :own], jnp.concatenate([low[:, :own], high[:, :own]]), last]


def add_terms(terms):
    return sum(term.astype(F32) for term in terms)


class Tokens:
    def __init__(self, heads_here):
        self.devices = lax.axis_size("tok")
        self.me = lax.axis_index("tok")
        self.heads = heads_here
        self.paired = self.devices == 8 and heads_here == 2
        self.group = self.devices // heads_here
        self.head = self.me // self.group
        self.quarter = self.me % self.group
        if self.paired:
            z, core = self.me // 2, self.me % 2
            chips = [z, 3 - z, z ^ 1, 3 - (z ^ 1)]
            self.order = jnp.stack(
                [c * 2 + core for c in chips] + [c * 2 + 1 - core for c in chips]
            )
            self.cuts = [(0, 4), (4, 4)]
            self.scatter_cuts = [(4, 4), (0, 4)]
        else:
            self.order = jnp.arange(self.devices)
            self.cuts = self.scatter_cuts = [(0, self.devices)]

    def swap(self, array_in, bits):
        return lax.ppermute(array_in, "tok", [(i, i ^ bits) for i in range(8)])

    def mirror(self, array_in):
        return lax.ppermute(array_in, "tok", [(i, 6 - 2 * (i // 2) + i % 2) for i in range(8)])

    def spread(self, order, by_head):
        by_head = order.tie(*by_head)
        if not self.paired:
            by_head = jnp.stack(by_head) if self.heads > 1 else by_head[None]
            everyone = lax.all_gather(by_head, "tok", axis=0)
            everyone = [lax.dynamic_index_in_dim(everyone, self.head, 1, False)]
            yield everyone
            yield everyone
            yield everyone
            return
        mine, other = by_head
        far, near = self.mirror(other), self.swap(mine, 2)
        yield
        last = self.swap(order.tie(far), 2)
        yield
        four = order.mark(jnp.stack(order.tie(mine, far, near, last)))
        yield [four, self.swap(four, 1)]

    def spread_same(self, array_in):
        if not self.paired:
            return lax.all_gather(array_in, "tok", axis=0)
        far = self.mirror(array_in)
        four = jnp.stack([array_in, far, self.swap(array_in, 2), self.swap(far, 2)])
        return jnp.concatenate([four, self.swap(four, 1)])

    def collect(self, order, merge):
        if not self.paired:
            blocks = order.tie((yield))
            shares = lax.all_to_all(blocks, "tok", split_axis=0, concat_axis=0, tiled=True)
            shares = shares.reshape((self.heads, self.group) + shares.shape[1:])
            yield
            merged = merge([shares[:, n] for n in range(self.group)])
            merged = [merged[n] for n in range(self.heads)]
            yield merged
            yield merged
            yield merged
            return
        got = self.swap(order.tie((yield)), 1)
        blocks = yield
        four = order.mark(merge(list(order.tie(blocks, got))))
        far = self.swap(four[3:], 2)
        yield
        far = order.mark(merge(list(order.tie(four[1:2], far))))
        far, near = self.mirror(far), self.swap(order.tie(four[2:3]), 2)
        yield
        own = order.mark(merge(list(order.tie(four[:1], near))))
        yield [own[0], far[0]]


def add_up(parts):
    total = parts[0].astype(F32)
    for part in parts[1:]:
        total = total + part.astype(F32)
    return total.astype(BF16)


def sum_everywhere(vector):
    if lax.axis_size("head") != 4 or lax.axis_size("tok") != 8:
        return lax.psum(vector, ("head", "tok"))
    for axis, count, bits in (
        ("tok", 8, 1), ("head", 4, 1), ("tok", 8, 2), ("head", 4, 2), ("tok", 8, 4),
    ):
        vector = vector + lax.ppermute(vector, axis, [(i, i ^ bits) for i in range(count)])
    return vector


def shards(
    stream_one,
    stream_two,
    buckets,
    lengths,
    gain_attn,
    bias_attn,
    qk_weight,
    value_weight,
    out_weight,
    gain_ffn,
    bias_ffn,
    in_weight,
    in_bias,
    down_weight,
    down_bias,
    cotangent_one,
    cotangent_two,
):
    tok_rows, shard_width = stream_one.shape
    head_devices = lax.axis_size("head")
    tok_devices = lax.axis_size("tok")
    me_head, me_tok = lax.axis_index("head"), lax.axis_index("tok")
    full_width = shard_width * head_devices
    hidden_width = in_bias.shape[0]
    heads = shard_width // DH
    tokens = Tokens(heads)
    per_device = 88
    plan = Plan(
        tok_devices, tok_rows, CAP // tok_devices, per_device * tok_devices // tokens.group
    )
    halves = [slice(h * plan.half, (h + 1) * plan.half) for h in range(HALVES)]

    order = Order()
    places = jnp.stack([me_head, tokens.head]).astype(jnp.int32)
    first_half, last_half = 0, HALVES - 1

    def head_columns(rows):
        if heads == 2:
            rows = [jnp.where(tokens.head == n, rows[1], rows[0]) for n in (1, 0)]
        return jnp.concatenate(rows, axis=1)

    vectors = jnp.stack([gain_attn, bias_attn, gain_ffn, bias_ffn])
    behind = jnp.concatenate([vectors, jnp.zeros((28, shard_width), BF16)])
    rows_in = [
        Steps(gather_features(order, jnp.concatenate([stream_two[halves[0]], behind]))),
        Steps(gather_features(order, stream_two[halves[1]])),
    ]
    rows_in[0].go()

    both_weights = jnp.concatenate(
        [
            weight[:, n * DH : (n + 1) * DH]
            for n in range(heads)
            for weight in (qk_weight, value_weight)
        ],
        axis=1,
    )
    whole_both = lax.all_gather(both_weights, "tok", axis=0, tiled=True)
    in_out = jnp.concatenate([in_weight, out_weight.T], axis=1)
    in_out = lax.all_gather(in_out, "tok", axis=0, tiled=True)

    names = jnp.concatenate(
        [buckets.T.astype(F32), jnp.full((8 - buckets.shape[1], tok_rows), -5.0, F32)]
    )
    named = tokens.spread_same(names)
    scalars = jnp.concatenate(
        [jnp.stack([tokens.quarter * plan.buckets]), tokens.order, lengths[:1]]
    ).astype(jnp.int32)
    ranks, since, empty = rank_call(plan, scalars, named)
    order.mark(since)
    rows_in[0].go()
    rows_in[1].go()
    ids = (me_tok * per_device + jnp.arange(per_device)).astype(F32)
    bucket_counts = order.mark(
        jnp.sum(
            (
                order.tie(named)[:, : buckets.shape[1]].reshape(1, -1) == ids[:, None]
            ).astype(jnp.int32),
            axis=1,
        )
    )

    pieces = [rows_in[0].result, None]
    by_distance = [piece[plan.half : plan.half + 8] for piece in pieces[0]]
    pieces[0] = [piece[: plan.half] for piece in pieces[0]]
    if len(by_distance) == 4:
        by_distance = jnp.stack(by_distance)
        by_distance = [
            lax.dynamic_index_in_dim(by_distance, me_head ^ n, 0, False) for n in range(4)
        ]
    vectors = jnp.concatenate(by_distance, axis=1).astype(F32)

    rows_two, normed, tables = [], [], []

    def project(h):
        one, *others = order.tie(*pieces[h]) if len(pieces[h]) > 1 else pieces[h]
        rows, normed_rows, *both = norm_call(
            places, [one, *others], vectors, whole_both, heads
        )
        rows_two.append(rows)
        normed.append(order.mark(normed_rows))
        tables.append(Steps(tokens.spread(order, both)))
        tables[h].go()

    slots = [[] for _ in tokens.cuts]

    def gather(h, n, found, call):
        found[n] = [order.mark(call(tokens.cuts[n][0], h, found[n]))]

    def gather_tables(first, h, more):
        n = [cut[0] for cut in tokens.cuts].index(first)
        return gather_call(plan, ranks, order.tie(tables[h].result[n]), first, h, more)

    rows_in[1].go()
    project(first_half)
    tables[0].go()
    pieces[1] = rows_in[1].result
    project(last_half)
    rows_stream = lax.all_gather(order.tie(stream_one), "head", axis=1, tiled=True)
    tables[0].go()
    gather(0, 0, slots, gather_tables)
    tables[1].go()
    if len(tokens.cuts) > 1:
        gather(0, 1, slots, gather_tables)
    tables[1].go()
    down_cols = lax.all_gather(order.tie(down_weight.T), "tok", axis=0, tiled=True)
    rows_grad = lax.all_gather(order.tie(cotangent_two), "head", axis=1, tiled=True)
    out_cols = lax.all_gather(
        order.tie(in_out[:, hidden_width:]), "head", axis=1, tiled=True
    )
    for n in range(len(tokens.cuts)):
        gather(1, n, slots, gather_tables)
    slots = [parts[0] for parts in slots]
    results, totals = attention_call(plan, scalars, slots, since, empty)
    order.mark(totals)

    def scatter(call, h, n):
        first, count = tokens.scatter_cuts[n]
        return order.mark(call(first, count, h))

    def scatter_forward(first, count, h):
        return scatter_call(plan, ranks, order.tie(results), totals, first, count, h)

    def collects(merge):
        made = []
        for _ in range(HALVES):
            steps = tokens.collect(order, merge)
            next(steps)
            made.append(steps)
        return made

    several = len(tokens.scatter_cuts) > 1
    mixing = collects(lambda parts: merge_call(plan, parts))
    part = scatter(scatter_forward, 0, 0)
    mixing[0].send(part)
    if several:
        part = scatter(scatter_forward, 0, 1)
        mixing[0].send(part)
    part = scatter(scatter_forward, 1, 0)
    mixing[1].send(part)
    next(mixing[0])
    if several:
        part = scatter(scatter_forward, 1, 1)
    mixed = [next(mixing[0])]

    def gather_attended(h):
        columns = head_columns([rows[: plan.half] for rows in mixed[h]])
        steps = Steps(gather_features(order, columns, h == last_half))
        steps.go()
        return steps

    attended_in = [gather_attended(0)]
    mixing[1].send(part if several else None)
    attended_in[0].go()
    next(mixing[1])
    mixed.append(next(mixing[1]))
    order.mark(*order.tie(*attended_in[0].result[::-1]))
    attended_in.append(gather_attended(1))
    attended_in[1].go()

    def feed_forward(h, before):
        pieces = attended_in[h].result
        pieces = list(order.tie(*pieces)) if len(pieces) > 1 else pieces
        kept = feed_forward_call(
            places,
            head_devices,
            h,
            rows_stream,
            pieces,
            rows_grad,
            cotangent_one,
            vectors,
            in_bias.astype(F32).reshape(1, -1),
            out_cols,
            in_out,
            down_cols,
            before,
        )
        order.mark(kept[7])
        return kept

    kept = feed_forward(0, [])
    sums, hidden_sums = kept[7:9]
    grad_sums = [Steps(sum_terms(order, kept[9:]))]
    grad_sums[0].go()
    kept = feed_forward(1, kept[:7])
    attended, result_one, normed_two, hidden, grad_pre, carried, second = kept[:7]
    sums, hidden_sums = sums + kept[7], hidden_sums + kept[8]
    grad_sums[0].go()
    grad_sums.append(Steps(sum_terms(order, kept[9:])))
    grad_sums[1].go()

    def pack(h):
        terms = grad_sums[h].result
        columns = [[t[:, n * DH : (n + 1) * DH] for t in terms] for n in range(heads)]
        if heads == 2:
            columns = [
                [jnp.where(tokens.head == n, b, a) for a, b in zip(*columns)] for n in (1, 0)
            ]
        columns[0][0] = order.tie(columns[0][0])
        packed = pack_call(plan, columns, mixed[h])
        order.mark(packed[0])
        steps = Steps(tokens.spread(order, packed))
        steps.go()
        return steps

    grad_slots = [[] for _ in tokens.cuts]

    def gather_grads(first, h, more):
        n = [cut[0] for cut in tokens.cuts].index(first)
        return gather_back_call(
            plan, scalars, ranks, order.tie(packed[h].result[n]), first, h, more
        )

    packed = [pack(0)]
    grad_down = order.mark(dot_tn(order.tie(hidden), rows_grad).astype(BF16))
    grad_sums[1].go()
    packed[0].go()
    grad_in = order.mark(dot_tn(order.tie(normed_two), grad_pre).astype(BF16))
    packed.append(pack(1))

    def over_tokens(part, axis):
        return lax.psum_scatter(
            part.astype(BF16), "tok", scatter_dimension=axis, tiled=True
        ).astype(F32)

    def over_heads(part):
        part = order.tie(part)
        return lax.psum_scatter(part, "head", scatter_dimension=1, tiled=True).astype(F32)

    packed[0].go()
    gather(0, 0, grad_slots, gather_grads)
    packed[1].go()
    grad_down, grad_in = order.tie(grad_down, grad_in)
    grad_down, grad_in = over_tokens(grad_down, 1), over_tokens(grad_in, 0)
    if len(tokens.cuts) > 1:
        gather(0, 1, grad_slots, gather_grads)
    packed[1].go()
    for n in range(len(tokens.cuts)):
        gather(1, n, grad_slots, gather_grads)
    grad_slots = [parts[0] for parts in grad_slots]
    grad_one = over_heads(carried).astype(BF16)

    slot_grads = order.mark(attention_back_call(plan, scalars, slots, grad_slots))
    second = over_heads(second)

    def scatter_back(first, count, h):
        return scatter_back_call(plan, ranks, order.tie(slot_grads), first, count, h)

    mixing = collects(add_up)
    part = scatter(scatter_back, 0, 0)
    mixing[0].send(part)
    if several:
        part = scatter(scatter_back, 0, 1)
        mixing[0].send(part)
    part = scatter(scatter_back, 1, 0)
    mixing[1].send(part)
    next(mixing[0])
    if several:
        part = scatter(scatter_back, 1, 1)
    grads = [next(mixing[0])]
    mixing[1].send(part if several else None)

    def project_back(h):
        *back_one, sums_one = norm_back_call(
            places, head_devices, rows_two[h], vectors, whole_both, list(order.tie(*grads[h]))
            if heads > 1
            else grads[h],
        )
        order.mark(sums_one)
        return back_one, sums_one

    grad_out = order.mark(dot_tn(order.tie(attended), grad_one).astype(BF16))
    if tokens.paired and head_devices == 4:
        grad_out = over_tokens(grad_out, 0).astype(BF16)
        own_part, other_part = [
            lax.ppermute(
                jnp.where(me_tok % 2 == n, grad_out[:, DH:], grad_out[:, :DH]),
                ("head", "tok"),
                [
                    (h * 8 + t, (t // 2) * 8 + 2 * h + (t + 1 - n) % 2)
                    for h in range(4)
                    for t in range(8)
                ],
            )
            for n in (1, 0)
        ]
        odd = me_tok % 2 == 1
        grad_out = jnp.concatenate(
            [jnp.where(odd, other_part, own_part), jnp.where(odd, own_part, other_part)]
        ).astype(F32)
    else:
        out_rows = lax.all_to_all(grad_out, "head", split_axis=0, concat_axis=1, tiled=True)
        grad_out = over_tokens(out_rows, 1)
    back_one, sums_one = project_back(0)
    last_steps = [Steps(sum_terms(order, back_one))]
    last_steps[0].go()
    next(mixing[1])
    grad_both = order.mark(dot_tn(normed[0], order.tie(head_columns(grads[0]))))
    last_steps[0].go()
    grads.append(next(mixing[1]))
    grad_both = grad_both + dot_tn(normed[1], order.tie(head_columns(grads[1])))
    grad_both = over_tokens(order.mark(grad_both.astype(BF16)), 0)
    back_one, sums_two = project_back(1)
    last_steps.append(Steps(sum_terms(order, back_one)))
    last_steps[1].go(2)
    grad_two = [
        (cotangent_two[rows].astype(F32) + add_terms(steps.result)).astype(BF16)
        for rows, steps in zip(halves, last_steps)
    ]
    result_two = (
        stream_two.astype(F32) + second + down_bias.astype(F32)
    ).astype(BF16)
    late = (sums_one + sums_two)[:2].reshape(-1)

    grad_qk, grad_value = [
        jnp.concatenate(
            [grad_both[:, n * DH : (n + 1) * DH] for n in range(first, 2 * heads, 2)], axis=1
        )
        for first in range(2)
    ]

    def place(part):
        whole = jnp.zeros((part.shape[0] * head_devices,), F32)
        return lax.dynamic_update_slice_in_dim(whole, part, me_head * part.shape[0], 0)

    def share(whole):
        size = whole.shape[0] // (head_devices * tok_devices)
        return lax.dynamic_slice_in_dim(whole, (me_head * tok_devices + me_tok) * size, size, 0)

    whole = sum_everywhere(
        jnp.concatenate(
            [
                sums[:2].reshape(-1),
                place(jnp.sum(cotangent_two.astype(F32), axis=0)),
                late,
                place(hidden_sums[0]),
            ]
        )
    )
    gain_two_sum, bias_two_sum, down_sum, gain_one_sum, bias_one_sum = [
        share(whole[n * full_width : (n + 1) * full_width]) for n in range(5)
    ]
    in_sum = share(whole[5 * full_width :])
    return (
        result_one,
        result_two,
        grad_one,
        jnp.concatenate(grad_two),
        gain_one_sum,
        bias_one_sum,
        grad_qk,
        grad_value,
        grad_out,
        gain_two_sum,
        bias_two_sum,
        grad_in,
        in_sum,
        grad_down,
        down_sum,
        bucket_counts,
    )


def solution(mesh):
    wide = P("tok", "head")
    placed = (
        wide, wide, P("tok", None), P(), P("head"), P("head"), wide, wide, P("head", "tok"),
        P("head"), P("head"), wide, P("head"), P("head", "tok"), P("head"), wide, wide,
    )
    vector = P(("head", "tok"))
    return jax.shard_map(
        shards,
        mesh=mesh,
        in_specs=placed,
        out_specs=(
            wide, wide, wide, wide, vector, vector, wide, wide, P("head", "tok"), vector, vector,
            wide, vector, P("head", "tok"), vector, P("tok"),
        ),
        check_vma=False,
    )
```
